128 devices in a mesh: grp: 4 (over x), scan: 32 (over z, y, core).
Axes of the slice: x: 4, y: 4, z: 4, core: 2. Of those that a mesh axis runs over, the one named last changes fastest.
Arguments:
- amplitude: float32 [512, 256, 256], P(('grp', 'scan')), may hold values from 0 to 3
- positions: int32 [512, 2], P(('grp', 'scan')), may hold values from 0 to 7936, as said below
- owner_perm: int32 [4, 32], replicated, may hold values from 0 to 31, each once within a row
- object_tiles: float32 [8192, 2, 4096], P(('grp', 'scan')), may hold values from -6 to 6
- probe: float32 [4, 2, 256, 256], P('grp'), may hold values from -6 to 6
Outputs:
- object_out: float32 [8192, 2, 4096], P(('grp', 'scan'))
- probe_out: float32 [4, 2, 256, 256], P('grp')
The draws below stay inside these ranges and needn't reach their ends.
Inputs may be any that keep to these rules, and one draw needn't show every extreme that they name: `positions`: each row is a pattern's top-left pixel (row, column), both multiples of 128. The 4 patterns of one device (consecutive rows) share their row and stand 2 * 64 pixels apart in column, the first leftmost. The patterns of group g of the grp axis lie inside tile rows g * 32 to (g + 1) * 32 - 1, and every window lies inside the object. `owner_perm`: row g maps the 32 owner classes of band g one to one onto the devices of the scan axis.
All inputs are finite; a program needn't handle non-finite values.
Results may differ from the reference program's by a relative error of at most 0.0003.
Values sent between devices are 32-bit elements; how exact they have to be, the bound alone decides.
No kernel may reach another device: no remote copies, remote signals or barrier semaphores. Data moves between devices by JAX's collectives and lax.ppermute only.
A program may use at most 128 MiB of HBM per device.

```python
import jax
import jax.numpy as jnp
from jax import lax

PATCH = 256
MODES = 4
PAT_DEV = 4
TILES_DEV = 64
OBJ_COLS = 64
ITERS = 2
TILE_SIDE = 64
BAND_ROWS = 32
COL_CLASSES = 4
STRIP_COLS = 10
PATTERNS = 512
TILES = 8192
N_GRP = 4
N_SCAN = 32


def draw_positions(key, part):
    key = jax.random.fold_in(key, 11)
    key_rows, key_first, key_second = jax.random.split(key, 3)
    devices_all = N_GRP * N_SCAN
    row_most = (BAND_ROWS - 4) // 2
    row_half = jax.random.randint(key_rows, (devices_all,), 0, row_most + 1)
    col_most = (OBJ_COLS - STRIP_COLS) // 2
    col_span = col_most + 1
    first_pick = jax.random.randint(key_first, (devices_all,), 0, col_span)
    second_pick = jax.random.randint(key_second, (devices_all,), 0, col_span)
    col_half = jnp.minimum(first_pick, second_pick)
    row_half = row_half.at[0].set(0).at[devices_all - 1].set(row_most)
    col_half = col_half.at[0].set(0).at[devices_all - 1].set(col_most)
    band = jnp.arange(devices_all, dtype=jnp.int32) // N_SCAN
    row_tile = band * BAND_ROWS + 2 * row_half
    steps_along = jnp.arange(PAT_DEV, dtype=jnp.int32)
    col_tile = 2 * col_half[:, None] + 2 * steps_along[None, :]
    rows_full = jnp.broadcast_to(row_tile[:, None], (devices_all, PAT_DEV))
    stacked = jnp.stack([rows_full * TILE_SIDE, col_tile * TILE_SIDE], axis=-1)
    return stacked.reshape(PATTERNS, 2).astype(jnp.int32)


def steps_of(stream_key, extent, shards, smallest, high):
    gain = 1.0
    for axis_at, blocks in shards:
        heights = jax.random.uniform(jax.random.fold_in(jax.random.fold_in(stream_key, 6), axis_at), (blocks,), jnp.float32, smallest / len(shards), high / len(shards))
        gain = gain * jnp.repeat(jnp.exp(heights), extent[axis_at] // blocks).reshape((-1,) + (1,) * (len(extent) - 1 - axis_at))
    return gain


def normal_values(rng, shape, width, limit, cuts=(), kind=jnp.bfloat16):
    factor_of = steps_of(rng, shape, cuts, -0.22, 0.18) if cuts else 1.0
    array = jax.random.normal(rng, shape, jnp.float32) * width * factor_of
    return jnp.minimum(jnp.maximum(array, -limit), limit).astype(kind)


def setup_inputs(seed: int = 0) -> dict:
    key_list = jax.random.split(jax.random.key(seed), 6)
    return {
        "amplitude": jnp.clip(3.0 * jax.random.uniform(key_list[0], (PATTERNS, PATCH, PATCH), jnp.float32) ** steps_of(key_list[0], (PATTERNS, PATCH, PATCH), ((0, 128),), -0.2, 0.2), 0.0, 3.0),
        "positions": draw_positions(jax.random.fold_in(key_list[5], 71), 0),
        "owner_perm": jax.vmap(lambda own: jax.random.permutation(own, N_SCAN))(jax.random.split(key_list[2], N_GRP)).reshape((N_GRP, N_SCAN)).astype(jnp.int32),
        "object_tiles": normal_values(key_list[3], (TILES, 2, TILE_SIDE * TILE_SIDE), 1.0, 6.0, ((0, 128),), jnp.float32),
        "probe": normal_values(key_list[4], (MODES, 2, PATCH, PATCH), 1.0, 6.0, ((0, 4),), jnp.float32),
    }


PROBE_STEP = 0.03125

def tile_index(positions, owner_perm):
    tile_side = PATCH // 4
    rows_top = positions[:, 0] // tile_side
    cols_left = positions[:, 1] // tile_side
    offsets = jnp.arange(4, dtype=jnp.int32)
    rows_all = rows_top[:, None, None] + offsets[None, :, None] + jnp.zeros((1, 1, 4), jnp.int32)
    cols_all = cols_left[:, None, None] + offsets[None, None, :] + jnp.zeros((1, 4, 1), jnp.int32)
    band = rows_all // BAND_ROWS
    within = rows_all - band * BAND_ROWS
    classes = within % 8 * COL_CLASSES + cols_all % COL_CLASSES
    owner_dev = owner_perm[band, classes]
    slot_num = within // 8 * (OBJ_COLS // COL_CLASSES) + cols_all // COL_CLASSES
    return ((band * N_SCAN + owner_dev) * TILES_DEV + slot_num).astype(jnp.int32)

def reference(amplitude, positions, owner_perm, object_tiles, probe):
    tile_side = PATCH // 4
    tile_area = tile_side * tile_side
    indices = tile_index(positions, owner_perm).reshape(PATTERNS, 16)
    current = object_tiles
    modes = probe
    for iteration in range(ITERS):
        probe_c = lax.complex(modes[:, 0], modes[:, 1])

        def one_pattern(carry, inputs):
            picks, measured = inputs
            window = current[picks].reshape(4, 4, 2, tile_side, tile_side)
            window = window.transpose(2, 0, 3, 1, 4).reshape(2, PATCH, PATCH)
            patch_c = lax.complex(window[0], window[1])
            exit_wave = probe_c * patch_c[None]
            far_field = jnp.fft.fft2(exit_wave, norm='ortho')
            intensity = lax.optimization_barrier(jnp.sum(jnp.real(far_field) ** 2 + jnp.imag(far_field) ** 2, axis=0))
            kept = far_field * (1.0 - measured / jnp.sqrt(intensity + 1.0))[None]
            chi_wave = jnp.fft.ifft2(kept, norm='ortho')
            object_part = lax.optimization_barrier(jnp.sum(jnp.conj(probe_c) * chi_wave, axis=0))
            probe_part = jnp.conj(patch_c)[None] * chi_wave
            probe_sum = carry + jnp.stack([jnp.real(probe_part), jnp.imag(probe_part)], axis=1)
            object_stack = jnp.stack([jnp.real(object_part), jnp.imag(object_part)], axis=0)
            object_cut = object_stack.reshape(2, 4, tile_side, 4, tile_side).transpose(1, 3, 0, 2, 4)
            return (probe_sum, object_cut.reshape(16, 2, tile_area))
        start = jnp.zeros((MODES, 2, PATCH, PATCH), jnp.float32)
        probe_grad, object_parts = lax.scan(one_pattern, start, (indices, amplitude))
        object_grad = jnp.zeros_like(current).at[indices.reshape(-1)].add(object_parts.reshape(-1, 2, tile_area))
        probe_peak = jnp.max(lax.optimization_barrier(jnp.sum(modes[:, 0] * modes[:, 0] + modes[:, 1] * modes[:, 1], axis=0))) + 1e-06
        current = current - object_grad / probe_peak
        modes = modes - probe_grad * PROBE_STEP
    return (current, modes)
```

```python
import functools
import math

import jax
import jax.numpy as jnp
import ml_dtypes
import numpy as np
from jax import lax
from jax.experimental import pallas as pl
from jax.experimental.pallas import tpu as pltpu
from jax.sharding import PartitionSpec as P

SIDE = 256
HALF = 128
TILE = 64
MODES = 4
PATS = 4
N_SCAN = 32
N_GRP = 4
BAND_ROWS = 32
GROUPS = 5
PROBE_STEP = 0.03125
OBJ_ROWS = 2 * GROUPS * 8
PRB_ROWS = 64
SEND_ROWS = OBJ_ROWS + PRB_ROWS
F32 = jnp.float32
BF16 = jnp.bfloat16


def row_of_position():
    return np.array([64 * r + 2 * q + h for r in range(2) for h in range(2) for q in range(32)])


def split_table(table):
    high = table.astype(ml_dtypes.bfloat16)
    low = (table - high.astype(np.float64)).astype(ml_dtypes.bfloat16)
    return high, low


def dft_tables():
    j = np.arange(HALF)[None, :]

    def real_form(n, odd):
        angle = 2.0 * math.pi * ((n[:, None] * (2 * j + odd)) % SIDE) / SIDE
        c, s = np.cos(angle) / 16.0, np.sin(angle) / 16.0
        return np.block([[c, -s], [s, c]])

    lanes = np.arange(HALF)
    rows = row_of_position()
    right, left = [], []
    for odd in (0, 1):
        for table in (real_form(lanes, odd), real_form(lanes, odd).T):
            high, low = split_table(table)
            right.append(np.concatenate([high, low, high], axis=0))
        for table in (real_form(rows, odd).T, real_form(rows, odd)):
            high, low = split_table(table)
            left.append(np.concatenate([high, low, high], axis=1))
    return np.stack(right), np.stack(left)


def split(x):
    high = x.astype(BF16)
    return high, (x - high.astype(F32)).astype(BF16)


def from_right(x, table):
    high, low = split(x)
    return jnp.dot(jnp.concatenate([high, high, low], axis=1), table, preferred_element_type=F32)


def from_left(table, x):
    high, low = split(x)
    return jnp.dot(table, jnp.concatenate([high, high, low], axis=0), preferred_element_type=F32)


def gradients(strip, probe, amp, right, left, far, sgrad, pgrad, weight):
    sgrad[...] = jnp.zeros_like(sgrad)
    pgrad[...] = jnp.zeros_like(pgrad)
    weight[...] = jnp.zeros_like(weight)

    def patch_block(p, c, rh, u):
        return strip[c, p + u, rh * HALF : (rh + 1) * HALF, :]

    def one_pattern(p, carry):
        bright = [None, None]
        for k in range(MODES):
            sums, diffs = [], []
            for rh in range(2):
                wave = []
                for u in range(2):
                    o_re, o_im = patch_block(p, 0, rh, u), patch_block(p, 1, rh, u)
                    p_re, p_im = probe[k, rh, 0, u], probe[k, rh, 1, u]
                    wave.append((p_re * o_re - p_im * o_im, p_re * o_im + p_im * o_re))
                sums.append(jnp.concatenate([wave[0][0] + wave[1][0], wave[0][1] + wave[1][1]], axis=1))
                diffs.append(jnp.concatenate([wave[0][0] - wave[1][0], wave[0][1] - wave[1][1]], axis=1))
            even = from_right(jnp.concatenate(sums, axis=0), right[0])
            odd = from_right(jnp.concatenate(diffs, axis=0), right[2])
            for eo in range(2):
                if eo == 0:
                    e, o = even[:HALF] + even[HALF:], odd[:HALF] + odd[HALF:]
                else:
                    e, o = even[:HALF] - even[HALF:], odd[:HALF] - odd[HALF:]
                stacked = jnp.concatenate(
                    [
                        jnp.concatenate([e[:, :HALF], o[:, :HALF]], axis=1),
                        jnp.concatenate([e[:, HALF:], o[:, HALF:]], axis=1),
                    ],
                    axis=0,
                )
                wave = from_left(left[2 * eo], stacked)
                far[k, eo] = wave
                power = wave[:HALF] * wave[:HALF] + wave[HALF:] * wave[HALF:]
                bright[eo] = power if k == 0 else bright[eo] + power
        scale = [amp[p, eo] * lax.rsqrt(bright[eo] + 1.0) for eo in range(2)]
        obj = {}
        for k in range(MODES):
            part = []
            for eo in range(2):
                wave = far[k, eo]
                cut = jnp.concatenate([wave[:HALF] * scale[eo], wave[HALF:] * scale[eo]], axis=0)
                part.append(from_left(left[2 * eo + 1], cut))
            top, low = part[0] + part[1], part[0] - part[1]
            rows_e = jnp.concatenate(
                [jnp.concatenate([w[:HALF, :HALF], w[HALF:, :HALF]], axis=1) for w in (top, low)], axis=0
            )
            rows_o = jnp.concatenate(
                [jnp.concatenate([w[:HALF, HALF:], w[HALF:, HALF:]], axis=1) for w in (top, low)], axis=0
            )
            even = from_right(rows_e, right[1])
            odd = from_right(rows_o, right[3])
            for u in range(2):
                psi = even + odd if u == 0 else even - odd
                for rh in range(2):
                    rows = slice(rh * HALF, (rh + 1) * HALF)
                    s_re, s_im = psi[rows, :HALF], psi[rows, HALF:]
                    o_re, o_im = patch_block(p, 0, rh, u), patch_block(p, 1, rh, u)
                    p_re, p_im = probe[k, rh, 0, u], probe[k, rh, 1, u]
                    g_re = p_re * s_re + p_im * s_im
                    g_im = p_re * s_im - p_im * s_re
                    if k == 0:
                        obj[u, rh] = (g_re, g_im)
                    else:
                        obj[u, rh] = (obj[u, rh][0] + g_re, obj[u, rh][1] + g_im)
                    pgrad[rh, k, 0, u] -= o_re * s_re + o_im * s_im
                    pgrad[rh, k, 1, u] -= o_re * s_im - o_im * s_re
        for u in range(2):
            for rh in range(2):
                o_re, o_im = patch_block(p, 0, rh, u), patch_block(p, 1, rh, u)
                power = 0.0
                for k in range(MODES):
                    p_re, p_im = probe[k, rh, 0, u], probe[k, rh, 1, u]
                    power = power + (p_re * p_re + p_im * p_im)
                rows = slice(rh * HALF, (rh + 1) * HALF)
                sgrad[0, p + u, rows, :] += power * o_re - obj[u, rh][0]
                sgrad[1, p + u, rows, :] += power * o_im - obj[u, rh][1]
                weight[rh, u] += o_re * o_re + o_im * o_im
        return carry

    lax.fori_loop(0, PATS, one_pattern, 0)
    for k in range(MODES):
        for rh in range(2):
            for c in range(2):
                for u in range(2):
                    pgrad[rh, k, c, u] += weight[rh, u] * probe[k, rh, c, u]


def peak_of(probe):
    most = None
    for rh in range(2):
        for u in range(2):
            power = 0.0
            for k in range(MODES):
                p_re, p_im = probe[k, rh, 0, u], probe[k, rh, 1, u]
                power = power + (p_re * p_re + p_im * p_im)
            most = power if most is None else jnp.maximum(most, power)
    return jnp.max(most) + 1e-6


def swap_halves(first, second):
    lane = lax.broadcasted_iota(jnp.int32, first.shape, 1)
    low = lane < TILE
    return (
        jnp.where(low, first, pltpu.roll(second, TILE, 1)),
        jnp.where(low, pltpu.roll(first, TILE, 1), second),
    )


def slot_of(info, perm, r, c):
    row, col = info[0] + r, info[1] + c
    return perm[(row % 8) * 4 + col % 4] * 3 + c // 4


def chunk_of(info, r, h, block):
    return ((info[0] + r) % 4) * 8 + h * 4 + block


def first_kernel(info, perm, tiles, probe, amp, right, left, strip, send, pgrad, peak, far, sgrad, weight):
    for r in range(4):
        for g in range(GROUPS):
            a, b = slot_of(info, perm, r, 2 * g), slot_of(info, perm, r, 2 * g + 1)
            for c in range(2):
                one = tiles[a, pl.ds(c, 32, stride=2), :]
                two = tiles[b, pl.ds(c, 32, stride=2), :]
                top, low = swap_halves(one, two)
                strip[c, g, 64 * r : 64 * r + 32, :] = top
                strip[c, g, 64 * r + 32 : 64 * r + 64, :] = low
    gradients(strip, probe, amp, right, left, far, sgrad, pgrad, weight)
    peak[0, 0] = peak_of(probe)
    for r in range(4):
        for h in range(2):
            for block in range(4):
                at = chunk_of(info, r, h, block)
                start = 64 * r + 32 * h + 8 * block
                for c in range(2):
                    for g in range(GROUPS):
                        line = (c * GROUPS + g) * 8
                        send[at, line : line + 8, :] = sgrad[c, g, start : start + 8, :]


def second_kernel(
    info, perm, peak, old_strip, first_send, total, other, old_probe, amp, right, left,
    out_tiles, pgrad, strip, probe, far, sgrad, weight
):
    inverse = 1.0 / peak[0, 0]
    for r in range(4):
        for h in range(2):
            for block in range(4):
                at = chunk_of(info, r, h, block)
                start = 64 * r + 32 * h + 8 * block
                for c in range(2):
                    for g in range(GROUPS):
                        line = (c * GROUPS + g) * 8
                        strip[c, g, start : start + 8, :] = (
                            old_strip[c, g, start : start + 8, :] - total[at, line : line + 8, :] * inverse
                        )
    mine = info[2]
    for k in range(MODES):
        for c in range(2):
            for u in range(2):
                for part in range(2):
                    piece = ((k * 2 + c) * 2 + u) * 2 + part
                    rows = slice(part * 64, part * 64 + 64)
                    probe[k, mine, c, u, rows, :] = (
                        old_probe[k, mine, c, u, rows, :] - total[piece, OBJ_ROWS:, :] * PROBE_STEP
                    )
                    probe[k, 1 - mine, c, u, rows, :] = (
                        old_probe[k, 1 - mine, c, u, rows, :] - other[piece] * PROBE_STEP
                    )
    gradients(strip, probe, amp, right, left, far, sgrad, pgrad, weight)
    inverse_now = 1.0 / peak_of(probe)
    for r in range(4):
        for g in range(GROUPS):
            a, b = slot_of(info, perm, r, 2 * g), slot_of(info, perm, r, 2 * g + 1)
            for c in range(2):
                lines = []
                for h in range(2):
                    start = 64 * r + 32 * h
                    line = (c * GROUPS + g) * 8
                    before = jnp.concatenate(
                        [first_send[chunk_of(info, r, h, block), line : line + 8, :] for block in range(4)], axis=0
                    )
                    lines.append(sgrad[c, g, start : start + 32, :] * inverse_now + before * inverse)
                one, two = swap_halves(lines[0], lines[1])
                out_tiles[a, pl.ds(c, 32, stride=2), :] = one
                out_tiles[b, pl.ds(c, 32, stride=2), :] = two


def served_slot(spots, mine, t, k):
    row, col = spots[t, 0], spots[t, 1]
    cls = mine[0]
    r = (cls // 4 - row + BAND_ROWS) % 8
    c = (cls % 4 - col + TILE) % 4 + 4 * k
    valid = jnp.logical_and(r < 4, c < 2 * GROUPS)
    slot = ((row + r) // 8) * 16 + (col + c) // 4
    return valid, jnp.where(valid, slot, 0)


def pack_kernel(spots, mine, tiles, out):
    def one(t, carry):
        for k in range(3):
            valid, slot = served_slot(spots, mine, t, k)
            out[t * 3 + k] = tiles[slot]
        return carry

    lax.fori_loop(0, N_SCAN, one, 0)


def unpack_kernel(spots, mine, tiles, arrived, out):
    out[...] = tiles[...]

    def one(t, carry):
        for k in range(3):
            valid, slot = served_slot(spots, mine, t, k)

            @pl.when(valid)
            def _():
                out[slot] -= arrived[t * 3 + k]

        return carry

    lax.fori_loop(0, N_SCAN, one, 0)


def owner_kernel(spots, me, arrived, out, band):
    band[...] = jnp.zeros_like(band)
    rho = me[0] // 8

    def place(t):
        row = spots[t, 0]
        r = row + (rho - row + BAND_ROWS) % 4
        return r // 4, spots[t, 1] // 2

    def add(t, carry):
        tr, lg = place(t)
        for c in range(2):
            for g in range(GROUPS):
                line = (c * GROUPS + g) * 8
                band[tr, c, lg + g] += arrived[t, line : line + 8, :]
        return carry

    def give(t, carry):
        tr, lg = place(t)
        for c in range(2):
            for g in range(GROUPS):
                line = (c * GROUPS + g) * 8
                out[t, line : line + 8, :] = band[tr, c, lg + g]
        return carry

    lax.fori_loop(0, N_SCAN, add, 0)
    lax.fori_loop(0, N_SCAN, give, 0)


def amplitude_kernel(amp, shuffle, out, moved):
    for p in range(PATS):
        x = amp[p]
        first = x.astype(BF16)
        rest = x - first.astype(F32)
        second = rest.astype(BF16)
        third = (rest - second.astype(F32)).astype(BF16)
        total = None
        for piece in (third, second, first):
            part = jnp.dot(piece, shuffle[...], preferred_element_type=F32)
            total = part if total is None else total + part
        for half in range(2):
            moved[half] = total[:, half * HALF : (half + 1) * HALF]
            for eo in range(2):
                out[p, eo, :, half * HALF : (half + 1) * HALF] = moved[half, pl.ds(eo, HALF, stride=2), :]


SMEM = pl.BlockSpec(memory_space=pltpu.SMEM)
VMEM = pl.BlockSpec(memory_space=pltpu.VMEM)


def kernel(body, outs, ins, scratch=(), out_specs=None, name=None):
    return pl.pallas_call(
        body,
        out_shape=outs,
        in_specs=ins,
        out_specs=out_specs if out_specs is not None else jax.tree.map(lambda _: VMEM, outs),
        scratch_shapes=list(scratch),
        compiler_params=pltpu.CompilerParams(vmem_limit_bytes=52 * 1024 * 1024),
        name=name,
    )


def shaped(*shape, dtype=F32):
    return jax.ShapeDtypeStruct(shape, dtype)


def shift(n, k):
    return [(i, (i + k) % n) for i in range(n)]


def shift_y(k):
    return [(i, (i & ~6) | ((((i >> 1) & 3) + k) % 4) << 1) for i in range(N_SCAN)]


def shift_z(k):
    return [(i, (i + 8 * k) % N_SCAN) for i in range(N_SCAN)]


SWAP = [(i, i ^ 1) for i in range(N_SCAN)]


def exchange(x):
    return lax.all_to_all(x, "scan", split_axis=0, concat_axis=0, tiled=True)


def scatter_sum(x, at, axis, perm_of):
    own = lax.dynamic_index_in_dim(x, at, 0, keepdims=False)
    for k in (1, 3, 2):
        row = lax.dynamic_index_in_dim(x, (at + k) % 4, 0, keepdims=False)
        own = own + lax.ppermute(row, axis, perm_of(k))
    return own


def gather_rows(x, at, axis, perm_of):
    stacked = jnp.zeros((4,) + x.shape, x.dtype)
    stacked = lax.dynamic_update_index_in_dim(stacked, x, at, 0)
    for k in (1, 3, 2):
        got = lax.ppermute(x, axis, perm_of(k))
        stacked = lax.dynamic_update_index_in_dim(stacked, got, (at - k) % 4, 0)
    return stacked


def body(amplitude, positions, owner_perm, object_tiles, probe):
    band = lax.axis_index("grp")
    me = lax.axis_index("scan")
    core, y_at, z_at = me % 2, me // 2 % 4, me // 8
    right_np, left_np = dft_tables()
    right, left = jnp.asarray(right_np), jnp.asarray(left_np)
    shuffle_np = np.zeros((SIDE, SIDE), np.float32)
    for m in range(SIDE):
        shuffle_np[m, m // 2 + HALF * (m % 2)] = 1.0
    shuffle = jnp.asarray(shuffle_np.astype(ml_dtypes.bfloat16))

    spot = positions[0] // TILE - jnp.array([BAND_ROWS, 0], jnp.int32) * band
    spots = exchange(jnp.broadcast_to(spot[None, None], (N_SCAN, 1, 2))).reshape(N_SCAN, 2)
    perm = lax.dynamic_index_in_dim(owner_perm, band, 0, keepdims=False)
    cls = jnp.sum(jnp.where(perm == me, jnp.arange(N_SCAN, dtype=jnp.int32), 0)).reshape(1)
    info = jnp.concatenate([spot, core.reshape(1).astype(jnp.int32)])
    place = me.reshape(1).astype(jnp.int32)

    tiles = object_tiles.reshape(TILE, 2, 32, HALF).transpose(0, 2, 1, 3).reshape(TILE, TILE, HALF)
    packed = kernel(pack_kernel, shaped(96, TILE, HALF), [SMEM, SMEM, VMEM], name="pack")(spots, cls, tiles)
    arrived = exchange(packed)

    own = probe.reshape(1, 2, 2, 2, 32, 2, 2, HALF).transpose(0, 2, 1, 6, 3, 5, 4, 7).reshape(1, 2, 2, 2, HALF, HALF)
    modes = lax.all_gather(own, "grp", axis=0, tiled=True)
    amp = kernel(amplitude_kernel, shaped(PATS, 2, HALF, SIDE), [VMEM, VMEM], [pltpu.VMEM((2, SIDE, HALF), F32)], name="spread")(amplitude, shuffle)

    scratch = [
        pltpu.VMEM((MODES, 2, SIDE, SIDE), F32),
        pltpu.VMEM((2, GROUPS, SIDE, HALF), F32),
        pltpu.VMEM((2, 2, HALF, HALF), F32),
    ]
    strip, send, pgrad, peak = kernel(
        first_kernel,
        (
            shaped(2, GROUPS, SIDE, HALF),
            shaped(N_SCAN, OBJ_ROWS, HALF),
            shaped(2, MODES, 2, 2, HALF, HALF),
            shaped(1, 1),
        ),
        [SMEM, SMEM] + [VMEM] * 5,
        scratch,
        out_specs=(VMEM, VMEM, VMEM, SMEM),
        name="first",
    )(info, perm, arrived, modes, amp, right, left)

    def chip_sum(x):
        kept = lax.dynamic_index_in_dim(x, core, 0, keepdims=False)
        given = lax.dynamic_index_in_dim(x, 1 - core, 0, keepdims=False)
        return kept + lax.ppermute(given, "scan", SWAP)

    chip = chip_sum(pgrad).reshape(N_SCAN, PRB_ROWS, HALF)
    got = exchange(jnp.concatenate([send, chip], axis=1))
    both = jnp.sum(got[:, OBJ_ROWS:].reshape(16, 2, PRB_ROWS, HALF), axis=0)
    summed = both
    for k in (1, 3, 2):
        summed = summed + lax.ppermute(both, "grp", shift(N_GRP, k))
    totals = kernel(
        owner_kernel,
        shaped(N_SCAN, OBJ_ROWS, HALF),
        [SMEM, SMEM, VMEM],
        [pltpu.VMEM((8, 2, 32, 8, HALF), F32)],
        name="owner",
    )(spots, place, got)
    answer = jnp.broadcast_to(summed[None], (16, 2, PRB_ROWS, HALF)).reshape(N_SCAN, PRB_ROWS, HALF)
    total = exchange(jnp.concatenate([totals, answer], axis=1))
    other = lax.ppermute(total[:, OBJ_ROWS:], "scan", SWAP)

    moved, pgrad = kernel(
        second_kernel,
        (shaped(96, TILE, HALF), shaped(2, MODES, 2, 2, HALF, HALF)),
        [SMEM, SMEM, SMEM] + [VMEM] * 8,
        [
            pltpu.VMEM((2, GROUPS, SIDE, HALF), F32),
            pltpu.VMEM((MODES, 2, 2, 2, HALF, HALF), F32),
        ]
        + scratch,
        name="second",
    )(info, perm, peak, strip, send, total, other, modes, amp, right, left)
    returned = exchange(moved)

    chip = chip_sum(pgrad)
    mine = scatter_sum(chip, band, "grp", lambda k: shift(N_GRP, k))
    mine = mine.reshape(4, 4, 32, HALF)
    mine = scatter_sum(mine, y_at, "scan", shift_y)
    mine = scatter_sum(mine, z_at, "scan", shift_z)
    mine = gather_rows(mine, z_at, "scan", shift_z)
    mine = gather_rows(mine, y_at, "scan", shift_y).reshape(2, 2, HALF, HALF)
    theirs = lax.ppermute(mine, "scan", SWAP)
    second_sum = jnp.where(core == 0, jnp.stack([mine, theirs]), jnp.stack([theirs, mine]))

    half_one = total[:, OBJ_ROWS:].reshape(MODES, 2, 2, HALF, HALF)
    half_one = lax.dynamic_index_in_dim(half_one, band, 0, keepdims=False)
    half_two = lax.dynamic_index_in_dim(other.reshape(MODES, 2, 2, HALF, HALF), band, 0, keepdims=False)
    first_sum = jnp.where(core == 0, jnp.stack([half_one, half_two]), jnp.stack([half_two, half_one]))
    probe_new = own[0] - first_sum * PROBE_STEP - second_sum * PROBE_STEP
    probe_out = (
        probe_new.reshape(2, 2, 2, 2, 2, 32, HALF).transpose(1, 0, 3, 5, 4, 2, 6).reshape(1, 2, SIDE, SIDE)
    )

    object_new = kernel(unpack_kernel, shaped(TILE, TILE, HALF), [SMEM, SMEM, VMEM, VMEM], name="unpack")(
        spots, cls, tiles, returned
    )
    object_out = object_new.reshape(TILE, 32, 2, HALF).transpose(0, 2, 1, 3).reshape(TILE, 2, TILE * TILE)
    return object_out, probe_out


def solution(mesh):
    in_specs = (
        P(("grp", "scan"), None, None),
        P(("grp", "scan"), None),
        P(),
        P(("grp", "scan"), None, None),
        P("grp", None, None, None),
    )
    out_specs = (P(("grp", "scan"), None, None), P("grp", None, None, None))
    return jax.shard_map(body, mesh=mesh, in_specs=in_specs, out_specs=out_specs, check_vma=False)
```

```python
import functools
import math

import jax
import jax.numpy as jnp
import ml_dtypes
import numpy as np
from jax import lax
from jax.experimental import pallas as pl
from jax.experimental.pallas import tpu as pltpu
from jax.sharding import PartitionSpec as P

SIDE = 256
HALF = 128
TILE = 64
MODES = 4
PATS = 4
N_SCAN = 32
N_GRP = 4
BAND_ROWS = 32
GROUPS = 5
PROBE_STEP = 0.03125
OBJ_ROWS = 2 * GROUPS * 8
PRB_ROWS = 64
SEND_ROWS = OBJ_ROWS + PRB_ROWS
WEAK = 0.1
F32 = jnp.float32
BF16 = jnp.bfloat16


def row_of_position():
    return np.array([64 * r + 2 * q + h for r in range(2) for h in range(2) for q in range(32)])


def split_table(table):
    high = table.astype(ml_dtypes.bfloat16)
    low = (table - high.astype(np.float64)).astype(ml_dtypes.bfloat16)
    return high, low


def dft_tables():
    j = np.arange(HALF)[None, :]

    def real_form(n, odd):
        angle = 2.0 * math.pi * ((n[:, None] * (2 * j + odd)) % SIDE) / SIDE
        c, s = np.cos(angle) / 16.0, np.sin(angle) / 16.0
        return np.block([[c, -s], [s, c]])

    lanes = np.arange(HALF)
    rows = row_of_position()
    right, left = [], []
    for odd in (0, 1):
        for table in (real_form(lanes, odd), real_form(lanes, odd).T):
            high, low = split_table(table)
            right.append(np.concatenate([high, low], axis=0))
        for table in (real_form(rows, odd).T, real_form(rows, odd)):
            high, low = split_table(table)
            left.append(np.concatenate([high, low], axis=1))
    return np.stack(right), np.stack(left)


def split(x):
    high = x.astype(BF16)
    return high, (x - high.astype(F32)).astype(BF16)


def product(first, second):
    return jnp.dot(first, second, preferred_element_type=F32)


def from_right(pair, at, table, fast):
    high = pair[at, 0]
    if fast:
        return product(high, table[:SIDE])
    return product(high, table[:SIDE]) + product(high, table[SIDE:]) + product(pair[at, 1], table[:SIDE])


def from_left(table, pair, at, fast):
    high = pair[at, 0]
    if fast:
        return product(table[:, :SIDE], high)
    return product(table[:, :SIDE], high) + product(table[:, SIDE:], high) + product(table[:, :SIDE], pair[at, 1])


CHUNK = 16


def chunks(count):
    return [slice(c * CHUNK, (c + 1) * CHUNK) for c in range(count // CHUNK)]


def woven(matrix_tasks, vector_tasks):
    total, done = len(vector_tasks), 0
    for i, task in enumerate(matrix_tasks):
        task()
        upto = total * (i + 1) // len(matrix_tasks)
        for piece in vector_tasks[done:upto]:
            piece()
        done = upto
    if not matrix_tasks:
        for piece in vector_tasks:
            piece()


def gradients(strip, probe, amp, right, left, work, fast):
    sgrad, pgrad, weight, strength = work["sgrad"], work["pgrad"], work["weight"], work["strength"]
    lhs, rhs, far, mid, res, bright = (work[n] for n in ("lhs", "rhs", "far", "mid", "res", "bright"))
    sgrad[...] = jnp.zeros_like(sgrad)
    pgrad[...] = jnp.zeros_like(pgrad)
    weight[...] = jnp.zeros_like(weight)

    def put_split(ref, at, rows, x):
        if fast:
            ref[at, 0, rows, :] = x.astype(BF16)
        else:
            ref[at, 0, rows, :], ref[at, 1, rows, :] = split(x)

    def one_pattern(p, carry):
        def exit_rows(k):
            def piece(rh, rows):
                full = slice(rh * HALF + rows.start, rh * HALF + rows.stop)
                wave = []
                for u in range(2):
                    o_re, o_im = strip[0, p + u, full, :], strip[1, p + u, full, :]
                    p_re, p_im = probe[k, rh, 0, u, rows, :], probe[k, rh, 1, u, rows, :]
                    wave.append((p_re * o_re - p_im * o_im, p_re * o_im + p_im * o_re))
                put_split(
                    lhs, 2 * (k % 2), full,
                    jnp.concatenate([wave[0][0] + wave[1][0], wave[0][1] + wave[1][1]], axis=1),
                )
                put_split(
                    lhs, 2 * (k % 2) + 1, full,
                    jnp.concatenate([wave[0][0] - wave[1][0], wave[0][1] - wave[1][1]], axis=1),
                )

            return [functools.partial(piece, rh, rows) for rh in range(2) for rows in chunks(HALF)]

        def right_dots(k, back):
            def one(eo):
                at = 2 * (k % 2) + eo
                res[at] = from_right(lhs, at, right[2 * eo + back], fast)

            return [functools.partial(one, eo) for eo in range(2)]

        def fold_rows(k):
            def piece(rows):
                low = slice(HALF + rows.start, HALF + rows.stop)
                at = 2 * (k % 2)
                e_top, e_low, o_top, o_low = res[at, rows, :], res[at, low, :], res[at + 1, rows, :], res[at + 1, low, :]
                for eo in range(2):
                    e = e_top + e_low if eo == 0 else e_top - e_low
                    o = o_top + o_low if eo == 0 else o_top - o_low
                    put_split(rhs, at + eo, rows, jnp.concatenate([e[:, :HALF], o[:, :HALF]], axis=1))
                    put_split(rhs, at + eo, low, jnp.concatenate([e[:, HALF:], o[:, HALF:]], axis=1))

            return [functools.partial(piece, rows) for rows in chunks(HALF)]

        def left_dots(k, back):
            def one(eo):
                at = 2 * (k % 2) + eo
                if back:
                    mid[at] = from_left(left[2 * eo + 1], rhs, at, fast)
                else:
                    far[k, eo] = from_left(left[2 * eo], rhs, at, fast)

            return [functools.partial(one, eo) for eo in range(2)]

        def power_rows(k):
            def piece(eo, rows):
                low = slice(HALF + rows.start, HALF + rows.stop)
                w_re, w_im = far[k, eo, rows, :], far[k, eo, low, :]
                power = w_re * w_re + w_im * w_im
                if k > 0:
                    power = bright[eo, rows, :] + power
                if k == MODES - 1:
                    power = amp[p, eo, rows, :] * lax.rsqrt(power + 1.0)
                bright[eo, rows, :] = power

            return [functools.partial(piece, eo, rows) for eo in range(2) for rows in chunks(HALF)]

        def cut_rows(k):
            def piece(eo, rows):
                low = slice(HALF + rows.start, HALF + rows.stop)
                scale = bright[eo, rows, :]
                put_split(rhs, 2 * (k % 2) + eo, rows, far[k, eo, rows, :] * scale)
                put_split(rhs, 2 * (k % 2) + eo, low, far[k, eo, low, :] * scale)

            return [functools.partial(piece, eo, rows) for eo in range(2) for rows in chunks(HALF)]

        def spread_rows(k):
            def piece(rows):
                low = slice(HALF + rows.start, HALF + rows.stop)
                at = 2 * (k % 2)
                for rh, full in enumerate((rows, low)):
                    if rh == 0:
                        w_re, w_im = mid[at, rows, :] + mid[at + 1, rows, :], mid[at, low, :] + mid[at + 1, low, :]
                    else:
                        w_re, w_im = mid[at, rows, :] - mid[at + 1, rows, :], mid[at, low, :] - mid[at + 1, low, :]
                    put_split(lhs, at, full, jnp.concatenate([w_re[:, :HALF], w_im[:, :HALF]], axis=1))
                    put_split(lhs, at + 1, full, jnp.concatenate([w_re[:, HALF:], w_im[:, HALF:]], axis=1))

            return [functools.partial(piece, rows) for rows in chunks(HALF)]

        def gradient_rows(k):
            def piece(rh, rows):
                full = slice(rh * HALF + rows.start, rh * HALF + rows.stop)
                at = 2 * (k % 2)
                even, odd = res[at, full, :], res[at + 1, full, :]
                for u in range(2):
                    psi = even + odd if u == 0 else even - odd
                    s_re, s_im = psi[:, :HALF], psi[:, HALF:]
                    o_re, o_im = strip[0, p + u, full, :], strip[1, p + u, full, :]
                    p_re, p_im = probe[k, rh, 0, u, rows, :], probe[k, rh, 1, u, rows, :]
                    g_re, g_im = p_re * s_re + p_im * s_im, p_re * s_im - p_im * s_re
                    if k == 0:
                        power = strength[rh, u, rows, :]
                        g_re, g_im = g_re - power * o_re, g_im - power * o_im
                    sgrad[0, p + u, full, :] -= g_re
                    sgrad[1, p + u, full, :] -= g_im
                    pgrad[rh, k, 0, u, rows, :] -= o_re * s_re + o_im * s_im
                    pgrad[rh, k, 1, u, rows, :] -= o_re * s_im - o_im * s_re
                    if k == 0:
                        weight[rh, u, rows, :] += o_re * o_re + o_im * o_im

            return [functools.partial(piece, rh, rows) for rh in range(2) for rows in chunks(HALF)]

        woven([], exit_rows(0))
        woven(right_dots(0, 0), exit_rows(1))
        woven(right_dots(1, 0), fold_rows(0))
        woven(left_dots(0, 0), exit_rows(2))
        woven(right_dots(2, 0), fold_rows(1) + power_rows(0))
        woven(left_dots(1, 0), exit_rows(3))
        woven(right_dots(3, 0), fold_rows(2) + power_rows(1))
        woven(left_dots(2, 0), fold_rows(3))
        woven(left_dots(3, 0), power_rows(2))
        woven([], power_rows(3) + cut_rows(0))
        woven(left_dots(0, 1), cut_rows(1))
        woven(left_dots(1, 1), spread_rows(0))
        woven(right_dots(0, 1), cut_rows(2))
        woven(left_dots(2, 1), spread_rows(1) + gradient_rows(0))
        woven(right_dots(1, 1), cut_rows(3))
        woven(left_dots(3, 1), spread_rows(2) + gradient_rows(1))
        woven(right_dots(2, 1), spread_rows(3))
        woven(right_dots(3, 1), gradient_rows(2))
        woven([], gradient_rows(3))
        return carry

    lax.fori_loop(0, PATS, one_pattern, 0)


WORK = {
    "sgrad": pltpu.VMEM((2, GROUPS, SIDE, HALF), F32),
    "pgrad": pltpu.VMEM((2, MODES, 2, 2, HALF, HALF), F32),
    "weight": pltpu.VMEM((2, 2, HALF, HALF), F32),
    "strength": pltpu.VMEM((2, 2, HALF, HALF), F32),
    "lhs": pltpu.VMEM((4, 2, SIDE, SIDE), BF16),
    "rhs": pltpu.VMEM((4, 2, SIDE, SIDE), BF16),
    "far": pltpu.VMEM((MODES, 2, SIDE, SIDE), F32),
    "mid": pltpu.VMEM((4, SIDE, SIDE), F32),
    "res": pltpu.VMEM((4, SIDE, SIDE), F32),
    "bright": pltpu.VMEM((2, HALF, SIDE), F32),
    "right": pltpu.VMEM((4, 2 * SIDE, SIDE), BF16),
    "left": pltpu.VMEM((4, SIDE, 2 * SIDE), BF16),
    "sems": pltpu.SemaphoreType.DMA((2,)),
}


def hand_over(info, probe, pgrad, weight, kept, given, turned):
    mine = info[2]
    for k in range(MODES):
        mode = (k + info[5]) & 3 if turned else k
        for block in range(4):
            at = (block + info[6]) & 3 if turned else block
            c, u = (at >> 1, at & 1) if turned else (block // 2, block % 2)
            for ref, rh in ((kept, mine), (given, 1 - mine)):
                ref[k, block // 2, block % 2] = pgrad[rh, mode, c, u] + weight[rh, u] * probe[mode, rh, c, u]


def probe_strength(probe, strength):
    most = None
    for rh in range(2):
        for u in range(2):
            for rows in chunks(HALF):
                power = 0.0
                for k in range(MODES):
                    p_re, p_im = probe[k, rh, 0, u, rows, :], probe[k, rh, 1, u, rows, :]
                    power = power + (p_re * p_re + p_im * p_im)
                strength[rh, u, rows, :] = power
                most = power if most is None else jnp.maximum(most, power)
    return jnp.max(most) + 1e-6


def weak_data(strip, strength, energy):
    weak = None
    for p in range(PATS):
        total = 0.0
        for rh in range(2):
            for u in range(2):
                for rows in chunks(HALF):
                    full = slice(rh * HALF + rows.start, rh * HALF + rows.stop)
                    o_re, o_im = strip[0, p + u, full, :], strip[1, p + u, full, :]
                    total = total + strength[rh, u, rows, :] * (o_re * o_re + o_im * o_im)
        small = energy[0, p] < WEAK * WEAK * jnp.sum(total)
        weak = small if weak is None else jnp.logical_and(weak, small)
    return weak


def swap_halves(first, second):
    lane = lax.broadcasted_iota(jnp.int32, first.shape, 1)
    low = lane < TILE
    return (
        jnp.where(low, first, pltpu.roll(second, TILE, 1)),
        jnp.where(low, pltpu.roll(first, TILE, 1), second),
    )


def slot_of(info, perm, r, c):
    row, col = info[0] + r, info[1] + c
    return perm[((row & 7) << 2) + (col & 3)] * 3 + c // 4


def chunk_of(info, r, h, block):
    return (((info[0] + r) & 3) << 3) + h * 4 + block


def start_tables(right_in, left_in, work):
    copies = [
        pltpu.make_async_copy(right_in, work["right"], work["sems"].at[0]),
        pltpu.make_async_copy(left_in, work["left"], work["sems"].at[1]),
    ]
    for copy in copies:
        copy.start()
    return copies


def first_kernel(
    info, perm, tiles, probe, amp, right_in, left_in, strip, send, kept, given, peak, *scratch
):
    work = dict(zip(WORK, scratch))
    sgrad, pgrad, weight = work["sgrad"], work["pgrad"], work["weight"]
    copies = start_tables(right_in, left_in, work)
    for r in range(4):
        for g in range(GROUPS):
            a, b = slot_of(info, perm, r, 2 * g), slot_of(info, perm, r, 2 * g + 1)
            for c in range(2):
                one = tiles[a, pl.ds(c, 32, stride=2), :]
                two = tiles[b, pl.ds(c, 32, stride=2), :]
                top, low = swap_halves(one, two)
                strip[c, g, 64 * r : 64 * r + 32, :] = top
                strip[c, g, 64 * r + 32 : 64 * r + 64, :] = low
    peak[0, 0] = probe_strength(probe, work["strength"])
    for copy in copies:
        copy.wait()
    gradients(strip, probe, amp, work["right"], work["left"], work, False)
    hand_over(info, probe, pgrad, weight, kept, given, False)
    for r in range(4):
        for h in range(2):
            for block in range(4):
                at = chunk_of(info, r, h, block)
                start = 64 * r + 32 * h + 8 * block
                for c in range(2):
                    for g in range(GROUPS):
                        line = (c * GROUPS + g) * 8
                        send[at, line : line + 8, :] = sgrad[c, g, start : start + 8, :]


def second_kernel(
    info, perm, peak, energy, old_strip, first_send, total, other, old_probe, amp, right_in, left_in,
    moved, kept_out, given_out, out_tiles, kept, given, out_sems, strip, probe, *scratch
):
    work = dict(zip(WORK, scratch))
    sgrad, pgrad, weight = work["sgrad"], work["pgrad"], work["weight"]
    copies = start_tables(right_in, left_in, work)
    inverse = 1.0 / peak[0, 0]
    for r in range(4):
        for h in range(2):
            for block in range(4):
                at = chunk_of(info, r, h, block)
                start = 64 * r + 32 * h + 8 * block
                for c in range(2):
                    for g in range(GROUPS):
                        line = (c * GROUPS + g) * 8
                        strip[c, g, start : start + 8, :] = (
                            old_strip[c, g, start : start + 8, :] - total[at, line : line + 8, :] * inverse
                        )
    mine = info[2]
    for k in range(MODES):
        for c in range(2):
            for u in range(2):
                for part in range(2):
                    piece = ((k * 2 + c) * 2 + u) * 2 + part
                    rows = slice(part * 64, part * 64 + 64)
                    probe[k, mine, c, u, rows, :] = (
                        old_probe[k, mine, c, u, rows, :] - total[piece, OBJ_ROWS:, :] * PROBE_STEP
                    )
                    probe[k, 1 - mine, c, u, rows, :] = (
                        old_probe[k, 1 - mine, c, u, rows, :] - other[piece] * PROBE_STEP
                    )
    inverse_now = 1.0 / probe_strength(probe, work["strength"])
    weak = weak_data(strip, work["strength"], energy)
    for copy in copies:
        copy.wait()

    @pl.when(weak)
    def _():
        gradients(strip, probe, amp, work["right"], work["left"], work, True)

    @pl.when(jnp.logical_not(weak))
    def _():
        gradients(strip, probe, amp, work["right"], work["left"], work, False)

    hand_over(info, probe, pgrad, weight, kept, given, True)
    out_copies = [
        pltpu.make_async_copy(given, given_out, out_sems.at[0]),
        pltpu.make_async_copy(kept, kept_out, out_sems.at[1]),
    ]
    for copy in out_copies:
        copy.start()
    for r in range(4):
        for g in range(GROUPS):
            a, b = slot_of(info, perm, r, 2 * g), slot_of(info, perm, r, 2 * g + 1)
            for c in range(2):
                lines = []
                for h in range(2):
                    start = 64 * r + 32 * h
                    line = (c * GROUPS + g) * 8
                    before = jnp.concatenate(
                        [first_send[chunk_of(info, r, h, block), line : line + 8, :] for block in range(4)], axis=0
                    )
                    lines.append(sgrad[c, g, start : start + 32, :] * inverse_now + before * inverse)
                one, two = swap_halves(lines[0], lines[1])
                out_tiles[r, 2 * g, pl.ds(c, 32, stride=2), :] = one
                out_tiles[r, 2 * g + 1, pl.ds(c, 32, stride=2), :] = two
            for col, at in ((2 * g, a), (2 * g + 1, b)):
                pltpu.make_async_copy(out_tiles.at[r, col], moved.at[at], out_sems.at[2]).start()
    for copy in out_copies:
        copy.wait()
    pltpu.make_async_copy(out_tiles, out_tiles, out_sems.at[2]).wait()


def spot_of(spots, t):
    return (spots[t, 0] >> 6) & (BAND_ROWS - 1), spots[t, 1] >> 6


def served_slot(spots, info, t, k):
    row, col = spot_of(spots, t)
    cls = info[4]
    r = ((cls >> 2) - row) & 7
    c = (((cls & 3) - col) & 3) + 4 * k
    valid = jnp.logical_and(r < 4, c < 2 * GROUPS)
    slot = (((row + r) >> 3) << 4) + ((col + c) >> 2)
    return valid, jnp.where(valid, slot, 0)


def pack_kernel(spots, info, tiles, out, sem):
    def one(t, carry):
        for k in range(3):
            valid, slot = served_slot(spots, info, t, k)
            pltpu.make_async_copy(tiles.at[slot], out.at[t * 3 + k], sem).start()
        return carry

    lax.fori_loop(0, N_SCAN, one, 0)
    pltpu.make_async_copy(out, out, sem).wait()


def unpack_kernel(spots, info, tiles, arrived, out):
    out[...] = tiles[...]

    def one(t, carry):
        for k in range(3):
            valid, slot = served_slot(spots, info, t, k)

            @pl.when(valid)
            def _():
                out[slot] -= arrived[t * 3 + k]

        return carry

    lax.fori_loop(0, N_SCAN, one, 0)


def owner_kernel(spots, info, arrived, out, band):
    band[...] = jnp.zeros_like(band)
    rho = info[3] >> 3

    def place(t):
        row, col = spot_of(spots, t)
        r = row + ((rho - row) & 3)
        return r >> 2, col >> 1

    def add(t, carry):
        tr, lg = place(t)
        for c in range(2):
            for g in range(GROUPS):
                line = (c * GROUPS + g) * 8
                band[tr, c, lg + g] += arrived[t, line : line + 8, :]
        return carry

    def give(t, carry):
        tr, lg = place(t)
        for c in range(2):
            for g in range(GROUPS):
                line = (c * GROUPS + g) * 8
                out[t, line : line + 8, :] = band[tr, c, lg + g]
        return carry

    lax.fori_loop(0, N_SCAN, add, 0)
    lax.fori_loop(0, N_SCAN, give, 0)


def chip_sums_kernel(arrived, out, rows, sem):
    copy = pltpu.make_async_copy(arrived.at[:, pl.ds(OBJ_ROWS, PRB_ROWS), :], rows, sem)
    copy.start()
    copy.wait()
    for core in range(2):
        for line in range(0, PRB_ROWS, 16):
            total = rows[core, line : line + 16, :]
            for chip in range(1, N_SCAN // 2):
                total = total + rows[2 * chip + core, line : line + 16, :]
            out[core, line : line + 16, :] = total


def finish_kernel(info, base, half, other_half, out, rows):
    for place, ref in ((0, half), (1, other_half)):
        rh = info[2] if place == 0 else 1 - info[2]
        for turn in range(4):
            at = (info[6] - turn) & 3
            c, u = at >> 1, at & 1
            for r in range(2):
                for h in range(2):
                    lines = slice(64 * r + 32 * h, 64 * r + 32 * h + 32)
                    new = base[rh, c, u, lines, :] - ref[turn, lines, :] * PROBE_STEP
                    rows[c, u, pl.ds(rh * HALF + (64 * r + h), 32, stride=2), :] = new
    for c in range(2):
        for u in range(2):
            out[0, c, :, u * HALF : (u + 1) * HALF] = rows[c, u]


def amplitude_kernel(amp, shuffle, out, energy, moved):
    for p in range(PATS):
        x = amp[p]
        energy[0, p] = jnp.sum(x * x)
        first = x.astype(BF16)
        rest = x - first.astype(F32)
        second = rest.astype(BF16)
        third = (rest - second.astype(F32)).astype(BF16)
        total = None
        for piece in (third, second, first):
            part = jnp.dot(piece, shuffle[...], preferred_element_type=F32)
            total = part if total is None else total + part
        for half in range(2):
            moved[half] = total[:, half * HALF : (half + 1) * HALF]
            for eo in range(2):
                out[p, eo, :, half * HALF : (half + 1) * HALF] = moved[half, pl.ds(eo, HALF, stride=2), :]


SMEM = pl.BlockSpec(memory_space=pltpu.SMEM)
VMEM = pl.BlockSpec(memory_space=pltpu.VMEM)
ANY = pl.BlockSpec(memory_space=pl.ANY)
HBM = pl.BlockSpec(memory_space=pltpu.HBM)


def kernel(body, outs, ins, scratch=(), out_specs=None, name=None, limit=20, cost=None):
    return pl.pallas_call(
        body,
        out_shape=outs,
        in_specs=ins,
        out_specs=out_specs if out_specs is not None else jax.tree.map(lambda _: VMEM, outs),
        scratch_shapes=list(scratch),
        compiler_params=pltpu.CompilerParams(vmem_limit_bytes=limit * 1024 * 1024),
        name=name,
        cost_estimate=None if cost is None else pl.CostEstimate(flops=0, bytes_accessed=cost, transcendentals=0),
    )


def shaped(*shape, dtype=F32):
    return jax.ShapeDtypeStruct(shape, dtype)


def shift(n, k):
    return [(i, (i + k) % n) for i in range(n)]


def shift_y(k):
    return [(i, (i & ~6) | ((((i >> 1) & 3) + k) % 4) << 1) for i in range(N_SCAN)]


def shift_z(k):
    return [(i, (i + 8 * k) % N_SCAN) for i in range(N_SCAN)]


SWAP = [(i, i ^ 1) for i in range(N_SCAN)]


def exchange(x):
    return lax.all_to_all(x, "scan", split_axis=0, concat_axis=0, tiled=True)


def sum_turned(parts, axis, perm_of):
    near, far, middle = (lax.ppermute(parts[k], axis, perm_of(k)) for k in (1, 3, 2))
    return (parts[0] + middle) + (near + far)


def sum_all(x, axis, perm_of):
    near, far, middle = (lax.ppermute(x, axis, perm_of(k)) for k in (1, 3, 2))
    return (x + middle) + (near + far)


def gather_rows(x, at, axis, perm_of):
    stacked = jnp.zeros((4,) + x.shape, x.dtype)
    stacked = lax.dynamic_update_index_in_dim(stacked, x, at, 0)
    for k in (1, 3, 2):
        got = lax.ppermute(x, axis, perm_of(k))
        stacked = lax.dynamic_update_index_in_dim(stacked, got, (at - k) % 4, 0)
    return stacked


def in_order(core, mine, theirs, axis):
    return jnp.where(core == 0, jnp.stack([mine, theirs], axis), jnp.stack([theirs, mine], axis))


def body(amplitude, positions, owner_perm, object_tiles, probe):
    band = lax.axis_index("grp")
    me = lax.axis_index("scan")
    core, y_at = me % 2, me // 2 % 4
    right_np, left_np = dft_tables()
    right, left = jnp.asarray(right_np), jnp.asarray(left_np)
    shuffle_np = np.zeros((SIDE, SIDE), np.float32)
    for m in range(SIDE):
        shuffle_np[m, m // 2 + HALF * (m % 2)] = 1.0
    shuffle = jnp.asarray(shuffle_np.astype(ml_dtypes.bfloat16))

    spots = exchange(jnp.broadcast_to(positions[:1, None], (N_SCAN, 1, 2))).reshape(N_SCAN, 2)
    perm = lax.dynamic_index_in_dim(owner_perm, band, 0, keepdims=False)
    cls = jnp.sum(jnp.where(perm == me, jnp.arange(N_SCAN, dtype=jnp.int32), 0))
    spot = positions[0] // TILE
    info = jnp.stack([spot[0] % BAND_ROWS, spot[1], core, me, cls, band, y_at]).astype(jnp.int32)

    tiles = object_tiles.reshape(TILE, 2, 32, HALF).transpose(0, 2, 1, 3).reshape(TILE, TILE, HALF)
    packed = kernel(
        pack_kernel,
        shaped(96, TILE, HALF),
        [SMEM, SMEM, HBM],
        [pltpu.SemaphoreType.DMA],
        out_specs=HBM,
        name="pack",
    )(spots, info, tiles)
    arrived = exchange(packed)

    own = probe.reshape(2, 2, 2, 32, 2, 2, HALF).transpose(1, 0, 5, 2, 4, 3, 6).reshape(2, 2, 2, HALF, HALF)
    part = gather_rows(lax.dynamic_index_in_dim(own, core, 0, keepdims=False), band, "grp", lambda k: shift(N_GRP, k))
    modes = in_order(core, part, lax.ppermute(part, "scan", SWAP), 1)
    amp, energy = kernel(
        amplitude_kernel,
        (shaped(PATS, 2, HALF, SIDE), shaped(1, PATS)),
        [VMEM, VMEM],
        [pltpu.VMEM((2, SIDE, HALF), F32)],
        out_specs=(VMEM, SMEM),
        name="spread",
    )(amplitude, shuffle)

    scratch = list(WORK.values())
    strip, send, kept, given, peak = kernel(
        first_kernel,
        (
            shaped(2, GROUPS, SIDE, HALF),
            shaped(N_SCAN, SEND_ROWS, HALF),
            shaped(MODES, 2, 2, HALF, HALF),
            shaped(MODES, 2, 2, HALF, HALF),
            shaped(1, 1),
        ),
        [SMEM, SMEM] + [VMEM] * 3 + [HBM] * 2,
        scratch,
        out_specs=(VMEM, VMEM, VMEM, VMEM, SMEM),
        name="first",
        limit=30,
    )(info, perm, arrived, modes, amp, right, left)

    chip = (kept + lax.ppermute(given, "scan", SWAP)).reshape(N_SCAN, PRB_ROWS, HALF)
    send = lax.dynamic_update_slice(send, chip, (0, OBJ_ROWS, 0))
    got = exchange(send)
    both = kernel(
        chip_sums_kernel,
        shaped(2, PRB_ROWS, HALF),
        [ANY],
        [pltpu.VMEM((N_SCAN, PRB_ROWS, HALF), F32), pltpu.SemaphoreType.DMA],
        name="sums",
    )(got)
    summed = sum_all(both, "grp", lambda k: shift(N_GRP, k))
    totals = kernel(
        owner_kernel,
        shaped(N_SCAN, SEND_ROWS, HALF),
        [SMEM, SMEM, VMEM],
        [pltpu.VMEM((8, 2, 32, 8, HALF), F32)],
        name="owner",
    )(spots, info, got)
    answer = jnp.broadcast_to(summed[None], (16, 2, PRB_ROWS, HALF)).reshape(N_SCAN, PRB_ROWS, HALF)
    total = exchange(lax.dynamic_update_slice(totals, answer, (0, OBJ_ROWS, 0)))
    other = lax.ppermute(total[:, OBJ_ROWS:], "scan", SWAP)

    moved, kept, given = kernel(
        second_kernel,
        (shaped(96, TILE, HALF), shaped(MODES, 2, 2, HALF, HALF), shaped(MODES, 2, 2, HALF, HALF)),
        [SMEM, SMEM, SMEM, SMEM] + [VMEM] * 6 + [HBM] * 2,
        [
            pltpu.VMEM((4, 2 * GROUPS, TILE, HALF), F32),
            pltpu.VMEM((MODES, 2, 2, HALF, HALF), F32),
            pltpu.VMEM((MODES, 2, 2, HALF, HALF), F32),
            pltpu.SemaphoreType.DMA((3,)),
            pltpu.VMEM((2, GROUPS, SIDE, HALF), F32),
            pltpu.VMEM((MODES, 2, 2, 2, HALF, HALF), F32),
        ]
        + scratch,
        out_specs=(HBM, HBM, HBM),
        name="second",
        limit=47,
    )(info, perm, peak, energy, strip, send, total, other, modes, amp, right, left)
    returned = exchange(moved)

    theirs = lax.ppermute(given, "scan", SWAP).reshape(4, 4, HALF, HALF)
    kept = kept.reshape(4, 4, HALF, HALF)
    mine = sum_turned([kept[k] + theirs[k] for k in range(4)], "grp", lambda k: shift(N_GRP, k))
    mine = sum_turned([mine[k] for k in range(4)], "scan", shift_y)
    mine = sum_all(mine, "scan", shift_z)
    object_new = kernel(
        unpack_kernel,
        shaped(TILE, TILE, HALF),
        [SMEM, SMEM, VMEM, VMEM],
        name="unpack",
        cost=8 * 1024 * 1024,
    )(spots, info, tiles, returned)
    mine, object_new = lax.optimization_barrier((mine, object_new))
    half = jnp.stack([mine] + [lax.ppermute(mine, "scan", shift_y(k)) for k in (1, 2, 3)])
    other_half = lax.ppermute(half, "scan", SWAP)

    half_one = total[:, OBJ_ROWS:].reshape(MODES, 2, 2, HALF, HALF)
    half_one = lax.dynamic_index_in_dim(half_one, band, 0, keepdims=False)
    half_two = lax.dynamic_index_in_dim(other.reshape(MODES, 2, 2, HALF, HALF), band, 0, keepdims=False)
    base = own - in_order(core, half_one, half_two, 0) * PROBE_STEP
    probe_out = kernel(
        finish_kernel,
        shaped(1, 2, SIDE, SIDE),
        [SMEM, VMEM, VMEM, VMEM],
        [pltpu.VMEM((2, 2, SIDE, HALF), F32)],
        name="finish",
    )(info, base, half, other_half)

    object_out = object_new.reshape(TILE, 32, 2, HALF).transpose(0, 2, 1, 3).reshape(TILE, 2, TILE * TILE)
    return object_out, probe_out


def solution(mesh):
    in_specs = (
        P(("grp", "scan"), None, None),
        P(("grp", "scan"), None),
        P(),
        P(("grp", "scan"), None, None),
        P("grp", None, None, None),
    )
    out_specs = (P(("grp", "scan"), None, None), P("grp", None, None, None))
    return jax.shard_map(body, mesh=mesh, in_specs=in_specs, out_specs=out_specs, check_vma=False)
```

```python
import functools
import math

import jax
import jax.numpy as jnp
import ml_dtypes
import numpy as np
from jax import lax
from jax.experimental import pallas as pl
from jax.experimental.pallas import tpu as pltpu
from jax.sharding import PartitionSpec as P

SIDE = 256
HALF = 128
TILE = 64
MODES = 4
PATS = 4
N_SCAN = 32
N_GRP = 4
BAND_ROWS = 32
GROUPS = 5
PROBE_STEP = 0.03125
OBJ_ROWS = 2 * GROUPS * 8
PRB_ROWS = 64
SEND_ROWS = OBJ_ROWS + PRB_ROWS
WEAK = 0.1
F32 = jnp.float32
BF16 = jnp.bfloat16


def row_of_position():
    return np.array([64 * r + 2 * q + h for r in range(2) for h in range(2) for q in range(32)])


def split_table(table):
    high = table.astype(ml_dtypes.bfloat16)
    low = (table - high.astype(np.float64)).astype(ml_dtypes.bfloat16)
    return high, low


def dft_tables():
    j = np.arange(HALF)[None, :]

    def real_form(n, odd):
        angle = 2.0 * math.pi * ((n[:, None] * (2 * j + odd)) % SIDE) / SIDE
        c, s = np.cos(angle) / 16.0, np.sin(angle) / 16.0
        return np.block([[c, -s], [s, c]])

    lanes = np.arange(HALF)
    rows = row_of_position()
    right, left = [], []
    for odd in (0, 1):
        for table in (real_form(lanes, odd), real_form(lanes, odd).T):
            high, low = split_table(table)
            right.append(np.concatenate([high, low], axis=0))
        for table in (real_form(rows, odd).T, real_form(rows, odd)):
            high, low = split_table(table)
            left.append(np.concatenate([high, low], axis=1))
    return np.stack(right), np.stack(left)


def split(x):
    high = x.astype(BF16)
    return high, (x - high.astype(F32)).astype(BF16)


def product(first, second):
    return jnp.dot(first, second, preferred_element_type=F32)


def from_right(pair, at, table, fast):
    high = pair[at, 0]
    if fast:
        return product(high, table[:SIDE])
    return product(high, table[:SIDE]) + product(high, table[SIDE:]) + product(pair[at, 1], table[:SIDE])


def from_left(table, pair, at, fast):
    high = pair[at, 0]
    if fast:
        return product(table[:, :SIDE], high)
    return product(table[:, :SIDE], high) + product(table[:, SIDE:], high) + product(table[:, :SIDE], pair[at, 1])


CHUNK = 16


def chunks(count):
    return [slice(c * CHUNK, (c + 1) * CHUNK) for c in range(count // CHUNK)]


def woven(matrix_tasks, vector_tasks):
    total, done = len(vector_tasks), 0
    for i, task in enumerate(matrix_tasks):
        task()
        upto = total * (i + 1) // len(matrix_tasks)
        for piece in vector_tasks[done:upto]:
            piece()
        done = upto
    if not matrix_tasks:
        for piece in vector_tasks:
            piece()


def gradients(strip, probe, amp, right, left, work, fast):
    sgrad, pgrad, weight, strength = work["sgrad"], work["pgrad"], work["weight"], work["strength"]
    lhs, rhs, far, mid, res, bright = (work[n] for n in ("lhs", "rhs", "far", "mid", "res", "bright"))
    sgrad[...] = jnp.zeros_like(sgrad)
    pgrad[...] = jnp.zeros_like(pgrad)
    weight[...] = jnp.zeros_like(weight)

    def put_split(ref, at, rows, x):
        if fast:
            ref[at, 0, rows, :] = x.astype(BF16)
        else:
            ref[at, 0, rows, :], ref[at, 1, rows, :] = split(x)

    def one_pattern(p, carry):
        def exit_rows(k):
            def piece(rh, rows):
                full = slice(rh * HALF + rows.start, rh * HALF + rows.stop)
                wave = []
                for u in range(2):
                    o_re, o_im = strip[0, p + u, full, :], strip[1, p + u, full, :]
                    p_re, p_im = probe[k, rh, 0, u, rows, :], probe[k, rh, 1, u, rows, :]
                    wave.append((p_re * o_re - p_im * o_im, p_re * o_im + p_im * o_re))
                put_split(
                    lhs, 2 * (k % 2), full,
                    jnp.concatenate([wave[0][0] + wave[1][0], wave[0][1] + wave[1][1]], axis=1),
                )
                put_split(
                    lhs, 2 * (k % 2) + 1, full,
                    jnp.concatenate([wave[0][0] - wave[1][0], wave[0][1] - wave[1][1]], axis=1),
                )

            return [functools.partial(piece, rh, rows) for rh in range(2) for rows in chunks(HALF)]

        def right_dots(k, back):
            def one(eo):
                at = 2 * (k % 2) + eo
                res[at] = from_right(lhs, at, right[2 * eo + back], fast)

            return [functools.partial(one, eo) for eo in range(2)]

        def fold_rows(k):
            def piece(rows):
                low = slice(HALF + rows.start, HALF + rows.stop)
                at = 2 * (k % 2)
                e_top, e_low, o_top, o_low = res[at, rows, :], res[at, low, :], res[at + 1, rows, :], res[at + 1, low, :]
                for eo in range(2):
                    e = e_top + e_low if eo == 0 else e_top - e_low
                    o = o_top + o_low if eo == 0 else o_top - o_low
                    put_split(rhs, at + eo, rows, jnp.concatenate([e[:, :HALF], o[:, :HALF]], axis=1))
                    put_split(rhs, at + eo, low, jnp.concatenate([e[:, HALF:], o[:, HALF:]], axis=1))

            return [functools.partial(piece, rows) for rows in chunks(HALF)]

        def left_dots(k, back):
            def one(eo):
                at = 2 * (k % 2) + eo
                if back:
                    mid[at] = from_left(left[2 * eo + 1], rhs, at, fast)
                else:
                    far[k, eo] = from_left(left[2 * eo], rhs, at, fast)

            return [functools.partial(one, eo) for eo in range(2)]

        def power_rows(k):
            def piece(eo, rows):
                low = slice(HALF + rows.start, HALF + rows.stop)
                w_re, w_im = far[k, eo, rows, :], far[k, eo, low, :]
                power = w_re * w_re + w_im * w_im
                if k > 0:
                    power = bright[eo, rows, :] + power
                if k == MODES - 1:
                    power = amp[p, eo, rows, :] * lax.rsqrt(power + 1.0)
                bright[eo, rows, :] = power

            return [functools.partial(piece, eo, rows) for eo in range(2) for rows in chunks(HALF)]

        def cut_rows(k):
            def piece(eo, rows):
                low = slice(HALF + rows.start, HALF + rows.stop)
                scale = bright[eo, rows, :]
                put_split(rhs, 2 * (k % 2) + eo, rows, far[k, eo, rows, :] * scale)
                put_split(rhs, 2 * (k % 2) + eo, low, far[k, eo, low, :] * scale)

            return [functools.partial(piece, eo, rows) for eo in range(2) for rows in chunks(HALF)]

        def spread_rows(k):
            def piece(rows):
                low = slice(HALF + rows.start, HALF + rows.stop)
                at = 2 * (k % 2)
                for rh, full in enumerate((rows, low)):
                    if rh == 0:
                        w_re, w_im = mid[at, rows, :] + mid[at + 1, rows, :], mid[at, low, :] + mid[at + 1, low, :]
                    else:
                        w_re, w_im = mid[at, rows, :] - mid[at + 1, rows, :], mid[at, low, :] - mid[at + 1, low, :]
                    put_split(lhs, at, full, jnp.concatenate([w_re[:, :HALF], w_im[:, :HALF]], axis=1))
                    put_split(lhs, at + 1, full, jnp.concatenate([w_re[:, HALF:], w_im[:, HALF:]], axis=1))

            return [functools.partial(piece, rows) for rows in chunks(HALF)]

        def gradient_rows(k):
            def piece(rh, rows):
                full = slice(rh * HALF + rows.start, rh * HALF + rows.stop)
                at = 2 * (k % 2)
                even, odd = res[at, full, :], res[at + 1, full, :]
                for u in range(2):
                    psi = even + odd if u == 0 else even - odd
                    s_re, s_im = psi[:, :HALF], psi[:, HALF:]
                    o_re, o_im = strip[0, p + u, full, :], strip[1, p + u, full, :]
                    p_re, p_im = probe[k, rh, 0, u, rows, :], probe[k, rh, 1, u, rows, :]
                    g_re, g_im = p_re * s_re + p_im * s_im, p_re * s_im - p_im * s_re
                    if k == 0:
                        power = strength[rh, u, rows, :]
                        g_re, g_im = g_re - power * o_re, g_im - power * o_im
                    sgrad[0, p + u, full, :] -= g_re
                    sgrad[1, p + u, full, :] -= g_im
                    pgrad[rh, k, 0, u, rows, :] -= o_re * s_re + o_im * s_im
                    pgrad[rh, k, 1, u, rows, :] -= o_re * s_im - o_im * s_re
                    if k == 0:
                        weight[rh, u, rows, :] += o_re * o_re + o_im * o_im

            return [functools.partial(piece, rh, rows) for rh in range(2) for rows in chunks(HALF)]

        woven([], exit_rows(0))
        woven(right_dots(0, 0), exit_rows(1))
        woven(right_dots(1, 0), fold_rows(0))
        woven(left_dots(0, 0), exit_rows(2))
        woven(right_dots(2, 0), fold_rows(1) + power_rows(0))
        woven(left_dots(1, 0), exit_rows(3))
        woven(right_dots(3, 0), fold_rows(2) + power_rows(1))
        woven(left_dots(2, 0), fold_rows(3))
        woven(left_dots(3, 0), power_rows(2))
        woven([], power_rows(3) + cut_rows(0))
        woven(left_dots(0, 1), cut_rows(1))
        woven(left_dots(1, 1), spread_rows(0))
        woven(right_dots(0, 1), cut_rows(2))
        woven(left_dots(2, 1), spread_rows(1) + gradient_rows(0))
        woven(right_dots(1, 1), cut_rows(3))
        woven(left_dots(3, 1), spread_rows(2) + gradient_rows(1))
        woven(right_dots(2, 1), spread_rows(3))
        woven(right_dots(3, 1), gradient_rows(2))
        woven([], gradient_rows(3))
        return carry

    lax.fori_loop(0, PATS, one_pattern, 0)


WORK = {
    "sgrad": pltpu.VMEM((2, GROUPS, SIDE, HALF), F32),
    "pgrad": pltpu.VMEM((2, MODES, 2, 2, HALF, HALF), F32),
    "weight": pltpu.VMEM((2, 2, HALF, HALF), F32),
    "strength": pltpu.VMEM((2, 2, HALF, HALF), F32),
    "lhs": pltpu.VMEM((4, 2, SIDE, SIDE), BF16),
    "rhs": pltpu.VMEM((4, 2, SIDE, SIDE), BF16),
    "far": pltpu.VMEM((MODES, 2, SIDE, SIDE), F32),
    "mid": pltpu.VMEM((4, SIDE, SIDE), F32),
    "res": pltpu.VMEM((4, SIDE, SIDE), F32),
    "bright": pltpu.VMEM((2, HALF, SIDE), F32),
    "right": pltpu.VMEM((4, 2 * SIDE, SIDE), BF16),
    "left": pltpu.VMEM((4, SIDE, 2 * SIDE), BF16),
    "needed": pltpu.VMEM((4, 2 * GROUPS, TILE, HALF), F32),
    "sems": pltpu.SemaphoreType.DMA((3,)),
}


def hand_over(info, probe, pgrad, weight, kept, given, turned):
    mine = info[2]
    for k in range(MODES):
        mode = (k + info[5]) & 3 if turned else k
        for block in range(4):
            at = (block + info[6]) & 3 if turned else block
            c, u = (at >> 1, at & 1) if turned else (block // 2, block % 2)
            for ref, rh in ((kept, mine), (given, 1 - mine)):
                ref[k, block // 2, block % 2] = pgrad[rh, mode, c, u] + weight[rh, u] * probe[mode, rh, c, u]


def probe_strength(probe, strength):
    most = None
    for rh in range(2):
        for u in range(2):
            for rows in chunks(HALF):
                power = 0.0
                for k in range(MODES):
                    p_re, p_im = probe[k, rh, 0, u, rows, :], probe[k, rh, 1, u, rows, :]
                    power = power + (p_re * p_re + p_im * p_im)
                strength[rh, u, rows, :] = power
                most = power if most is None else jnp.maximum(most, power)
    return jnp.max(most) + 1e-6


def weak_data(strip, strength, energy):
    weak = None
    for p in range(PATS):
        total = 0.0
        for rh in range(2):
            for u in range(2):
                for rows in chunks(HALF):
                    full = slice(rh * HALF + rows.start, rh * HALF + rows.stop)
                    o_re, o_im = strip[0, p + u, full, :], strip[1, p + u, full, :]
                    total = total + strength[rh, u, rows, :] * (o_re * o_re + o_im * o_im)
        small = energy[0, p] < WEAK * WEAK * jnp.sum(total)
        weak = small if weak is None else jnp.logical_and(weak, small)
    return weak


def swap_halves(first, second):
    lane = lax.broadcasted_iota(jnp.int32, first.shape, 1)
    low = lane < TILE
    return (
        jnp.where(low, first, pltpu.roll(second, TILE, 1)),
        jnp.where(low, pltpu.roll(first, TILE, 1), second),
    )


def slot_of(info, perm, r, c):
    row, col = info[0] + r, info[1] + c
    return perm[((row & 7) << 2) + (col & 3)] * 3 + c // 4


def chunk_of(info, r, h, block):
    return (((info[0] + r) & 3) << 3) + h * 4 + block


def start_tables(right_in, left_in, work):
    copies = [
        pltpu.make_async_copy(right_in, work["right"], work["sems"].at[0]),
        pltpu.make_async_copy(left_in, work["left"], work["sems"].at[1]),
    ]
    for copy in copies:
        copy.start()
    return copies


def first_kernel(
    info, perm, tiles, probe, amp, right_in, left_in, strip, send, kept, given, peak, *scratch
):
    work = dict(zip(WORK, scratch))
    sgrad, pgrad, weight = work["sgrad"], work["pgrad"], work["weight"]
    needed, sem = work["needed"], work["sems"].at[2]
    for r in range(4):
        for c in range(2 * GROUPS):
            pltpu.make_async_copy(tiles.at[slot_of(info, perm, r, c)], needed.at[r, c], sem).start()
    copies = start_tables(right_in, left_in, work)
    peak[0, 0] = probe_strength(probe, work["strength"])
    pltpu.make_async_copy(needed, needed, sem).wait()
    for r in range(4):
        for g in range(GROUPS):
            for c in range(2):
                one = needed[r, 2 * g, pl.ds(c, 32, stride=2), :]
                two = needed[r, 2 * g + 1, pl.ds(c, 32, stride=2), :]
                top, low = swap_halves(one, two)
                strip[c, g, 64 * r : 64 * r + 32, :] = top
                strip[c, g, 64 * r + 32 : 64 * r + 64, :] = low
    for copy in copies:
        copy.wait()
    gradients(strip, probe, amp, work["right"], work["left"], work, False)
    hand_over(info, probe, pgrad, weight, kept, given, False)
    for r in range(4):
        for h in range(2):
            for block in range(4):
                at = chunk_of(info, r, h, block)
                start = 64 * r + 32 * h + 8 * block
                for c in range(2):
                    for g in range(GROUPS):
                        line = (c * GROUPS + g) * 8
                        send[at, line : line + 8, :] = sgrad[c, g, start : start + 8, :]


def second_kernel(
    info, perm, peak, energy, old_strip, first_in, total_in, other_in, old_probe, amp, right_in, left_in,
    moved, kept_out, given_out, kept, given, out_sems, strip, probe, first_send, total, other, in_sems, *scratch
):
    work = dict(zip(WORK, scratch))
    sgrad, pgrad, weight, out_tiles = work["sgrad"], work["pgrad"], work["weight"], work["needed"]
    pairs = ((old_strip, strip), (total_in, total), (old_probe, probe), (other_in, other), (first_in, first_send))
    come = [pltpu.make_async_copy(a, b, in_sems.at[i]) for i, (a, b) in enumerate(pairs)]
    for copy in come:
        copy.start()
    copies = start_tables(right_in, left_in, work)
    inverse = 1.0 / peak[0, 0]
    come[0].wait()
    come[1].wait()
    for r in range(4):
        for h in range(2):
            for block in range(4):
                at = chunk_of(info, r, h, block)
                start = 64 * r + 32 * h + 8 * block
                for c in range(2):
                    for g in range(GROUPS):
                        line = (c * GROUPS + g) * 8
                        strip[c, g, start : start + 8, :] -= total[at, line : line + 8, :] * inverse
    mine = info[2]
    come[2].wait()
    come[3].wait()
    for k in range(MODES):
        for c in range(2):
            for u in range(2):
                for part in range(2):
                    piece = ((k * 2 + c) * 2 + u) * 2 + part
                    rows = slice(part * 64, part * 64 + 64)
                    probe[k, mine, c, u, rows, :] -= total[piece, OBJ_ROWS:, :] * PROBE_STEP
                    probe[k, 1 - mine, c, u, rows, :] -= other[piece] * PROBE_STEP
    inverse_now = 1.0 / probe_strength(probe, work["strength"])
    weak = weak_data(strip, work["strength"], energy)
    for copy in copies:
        copy.wait()

    @pl.when(weak)
    def _():
        gradients(strip, probe, amp, work["right"], work["left"], work, True)

    @pl.when(jnp.logical_not(weak))
    def _():
        gradients(strip, probe, amp, work["right"], work["left"], work, False)

    hand_over(info, probe, pgrad, weight, kept, given, True)
    out_copies = [
        pltpu.make_async_copy(given, given_out, out_sems.at[0]),
        pltpu.make_async_copy(kept, kept_out, out_sems.at[1]),
    ]
    for copy in out_copies:
        copy.start()
    come[4].wait()
    for r in range(4):
        for g in range(GROUPS):
            a, b = slot_of(info, perm, r, 2 * g), slot_of(info, perm, r, 2 * g + 1)
            for c in range(2):
                lines = []
                for h in range(2):
                    start = 64 * r + 32 * h
                    line = (c * GROUPS + g) * 8
                    before = jnp.concatenate(
                        [first_send[chunk_of(info, r, h, block), line : line + 8, :] for block in range(4)], axis=0
                    )
                    lines.append(sgrad[c, g, start : start + 32, :] * inverse_now + before * inverse)
                one, two = swap_halves(lines[0], lines[1])
                out_tiles[r, 2 * g, pl.ds(c, 32, stride=2), :] = one
                out_tiles[r, 2 * g + 1, pl.ds(c, 32, stride=2), :] = two
            for col, at in ((2 * g, a), (2 * g + 1, b)):
                pltpu.make_async_copy(out_tiles.at[r, col], moved.at[at], out_sems.at[2]).start()
    for copy in out_copies:
        copy.wait()
    pltpu.make_async_copy(out_tiles, out_tiles, out_sems.at[2]).wait()


def spot_of(spots, t):
    return (spots[t, 0] >> 6) & (BAND_ROWS - 1), spots[t, 1] >> 6


def own_class(info, perm):
    return lax.fori_loop(0, N_SCAN, lambda i, found: jnp.where(perm[i] == info[3], i, found), 0)


def served_slot(spots, cls, t, k):
    row, col = spot_of(spots, t)
    r = ((cls >> 2) - row) & 7
    c = (((cls & 3) - col) & 3) + 4 * k
    valid = jnp.logical_and(r < 4, c < 2 * GROUPS)
    slot = (((row + r) >> 3) << 4) + ((col + c) >> 2)
    return valid, jnp.where(valid, slot, 0)


def pack_kernel(spots, info, perm, tiles, out, sem):
    cls = own_class(info, perm)

    def one(t, carry):
        for k in range(3):
            _, slot = served_slot(spots, cls, t, k)
            pltpu.make_async_copy(tiles.at[slot], out.at[t * 3 + k], sem).start()
        return carry

    lax.fori_loop(0, N_SCAN, one, 0)
    pltpu.make_async_copy(out, out, sem).wait()


PARTS = 4


def unpack_kernel(spots, info, perm, tiles, arrived, out, total, came, sems):
    cls = own_class(info, perm)
    step = N_SCAN // PARTS
    held = total.at[pl.ds(0, TILE)]
    pltpu.make_async_copy(tiles, held, sems.at[PARTS]).start()
    parts = []
    for part in range(PARTS):
        rows = pl.ds(part * step * 3, step * 3)
        parts.append(pltpu.make_async_copy(arrived.at[rows], came.at[rows], sems.at[part]))
        parts[-1].start()
    pltpu.make_async_copy(tiles, held, sems.at[PARTS]).wait()
    total[TILE] = jnp.zeros((TILE, HALF), F32)

    def one(t, carry):
        for k in range(3):
            valid, slot = served_slot(spots, cls, t, k)
            at = jnp.where(valid, slot, TILE)
            total[at] -= came[t * 3 + k]
        return carry

    for part in range(PARTS):
        parts[part].wait()
        lax.fori_loop(part * step, (part + 1) * step, one, 0)
    last = pltpu.make_async_copy(held, out, sems.at[PARTS])
    last.start()
    last.wait()


def owner_kernel(spots, info, arrived, out, band):
    band[...] = jnp.zeros_like(band)
    rho = info[3] >> 3

    def place(t):
        row, col = spot_of(spots, t)
        r = row + ((rho - row) & 3)
        return r >> 2, col >> 1

    def add(t, carry):
        tr, lg = place(t)
        for c in range(2):
            for g in range(GROUPS):
                line = (c * GROUPS + g) * 8
                band[tr, c, lg + g] += arrived[t, line : line + 8, :]
        return carry

    def give(t, carry):
        tr, lg = place(t)
        for c in range(2):
            for g in range(GROUPS):
                line = (c * GROUPS + g) * 8
                out[t, line : line + 8, :] = band[tr, c, lg + g]
        return carry

    lax.fori_loop(0, N_SCAN, add, 0)
    lax.fori_loop(0, N_SCAN, give, 0)


def chip_sums_kernel(arrived, out, rows, sem):
    copy = pltpu.make_async_copy(arrived.at[:, pl.ds(OBJ_ROWS, PRB_ROWS), :], rows, sem)
    copy.start()
    copy.wait()
    for core in range(2):
        for line in range(0, PRB_ROWS, 16):
            total = rows[core, line : line + 16, :]
            for chip in range(1, N_SCAN // 2):
                total = total + rows[2 * chip + core, line : line + 16, :]
            out[core, line : line + 16, :] = total


def finish_kernel(info, base, half, other_half, out, rows):
    for place, ref in ((0, half), (1, other_half)):
        rh = info[2] if place == 0 else 1 - info[2]
        for turn in range(4):
            at = (info[6] - turn) & 3
            c, u = at >> 1, at & 1
            for r in range(2):
                for h in range(2):
                    lines = slice(64 * r + 32 * h, 64 * r + 32 * h + 32)
                    new = base[rh, c, u, lines, :] - ref[turn, lines, :] * PROBE_STEP
                    rows[c, u, pl.ds(rh * HALF + (64 * r + h), 32, stride=2), :] = new
    for c in range(2):
        for u in range(2):
            out[0, c, :, u * HALF : (u + 1) * HALF] = rows[c, u]


def amplitude_kernel(amp, shuffle, out, energy, moved):
    for p in range(PATS):
        x = amp[p]
        energy[0, p] = jnp.sum(x * x)
        first = x.astype(BF16)
        rest = x - first.astype(F32)
        second = rest.astype(BF16)
        third = (rest - second.astype(F32)).astype(BF16)
        total = None
        for piece in (third, second, first):
            part = jnp.dot(piece, shuffle[...], preferred_element_type=F32)
            total = part if total is None else total + part
        for half in range(2):
            moved[half] = total[:, half * HALF : (half + 1) * HALF]
            for eo in range(2):
                out[p, eo, :, half * HALF : (half + 1) * HALF] = moved[half, pl.ds(eo, HALF, stride=2), :]


SMEM = pl.BlockSpec(memory_space=pltpu.SMEM)
VMEM = pl.BlockSpec(memory_space=pltpu.VMEM)
ANY = pl.BlockSpec(memory_space=pl.ANY)
HBM = pl.BlockSpec(memory_space=pltpu.HBM)


def kernel(body, outs, ins, scratch=(), out_specs=None, name=None, limit=20, cost=None):
    return pl.pallas_call(
        body,
        out_shape=outs,
        in_specs=ins,
        out_specs=out_specs if out_specs is not None else jax.tree.map(lambda _: VMEM, outs),
        scratch_shapes=list(scratch),
        compiler_params=pltpu.CompilerParams(vmem_limit_bytes=limit * 1024 * 1024),
        name=name,
        cost_estimate=None if cost is None else pl.CostEstimate(flops=0, bytes_accessed=cost, transcendentals=0),
    )


def shaped(*shape, dtype=F32):
    return jax.ShapeDtypeStruct(shape, dtype)


def shift(n, k):
    return [(i, (i + k) % n) for i in range(n)]


def shift_y(k):
    return [(i, (i & ~6) | ((((i >> 1) & 3) + k) % 4) << 1) for i in range(N_SCAN)]


def shift_z(k):
    return [(i, (i + 8 * k) % N_SCAN) for i in range(N_SCAN)]


SWAP = [(i, i ^ 1) for i in range(N_SCAN)]


def exchange(x):
    return lax.all_to_all(x, "scan", split_axis=0, concat_axis=0, tiled=True)


def sum_turned(parts, axis, perm_of):
    near, far, middle = (lax.ppermute(parts[k], axis, perm_of(k)) for k in (1, 3, 2))
    return (parts[0] + middle) + (near + far)


def sum_all(x, axis, perm_of):
    near, far, middle = (lax.ppermute(x, axis, perm_of(k)) for k in (1, 3, 2))
    return (x + middle) + (near + far)


def gather_rows(x, at, axis, perm_of):
    stacked = jnp.zeros((4,) + x.shape, x.dtype)
    stacked = lax.dynamic_update_index_in_dim(stacked, x, at, 0)
    for k in (1, 3, 2):
        got = lax.ppermute(x, axis, perm_of(k))
        stacked = lax.dynamic_update_index_in_dim(stacked, got, (at - k) % 4, 0)
    return stacked


def in_order(core, mine, theirs, axis):
    return jnp.where(core == 0, jnp.stack([mine, theirs], axis), jnp.stack([theirs, mine], axis))


def body(amplitude, positions, owner_perm, object_tiles, probe):
    band = lax.axis_index("grp")
    me = lax.axis_index("scan")
    core, y_at = me % 2, me // 2 % 4
    right_np, left_np = dft_tables()
    right, left = jnp.asarray(right_np), jnp.asarray(left_np)
    shuffle_np = np.zeros((SIDE, SIDE), np.float32)
    for m in range(SIDE):
        shuffle_np[m, m // 2 + HALF * (m % 2)] = 1.0
    shuffle = jnp.asarray(shuffle_np.astype(ml_dtypes.bfloat16))

    spots = exchange(jnp.broadcast_to(positions[:1, None], (N_SCAN, 1, 2))).reshape(N_SCAN, 2)
    perm = lax.dynamic_index_in_dim(owner_perm, band, 0, keepdims=False)
    spot = positions[0] // TILE
    info = jnp.stack([spot[0] % BAND_ROWS, spot[1], core, me, me, band, y_at]).astype(jnp.int32)

    tiles = object_tiles.reshape(TILE, 2, 32, HALF).transpose(0, 2, 1, 3).reshape(TILE, TILE, HALF)
    packed = kernel(
        pack_kernel,
        shaped(96, TILE, HALF),
        [SMEM, SMEM, SMEM, HBM],
        [pltpu.SemaphoreType.DMA],
        out_specs=HBM,
        name="pack",
    )(spots, info, perm, tiles)
    arrived = exchange(packed)

    own = probe.reshape(2, 2, 2, 32, 2, 2, HALF).transpose(1, 0, 5, 2, 4, 3, 6).reshape(2, 2, 2, HALF, HALF)
    part = gather_rows(lax.dynamic_index_in_dim(own, core, 0, keepdims=False), band, "grp", lambda k: shift(N_GRP, k))
    modes = in_order(core, part, lax.ppermute(part, "scan", SWAP), 1)
    amp, energy = kernel(
        amplitude_kernel,
        (shaped(PATS, 2, HALF, SIDE), shaped(1, PATS)),
        [VMEM, VMEM],
        [pltpu.VMEM((2, SIDE, HALF), F32)],
        out_specs=(VMEM, SMEM),
        name="spread",
    )(amplitude, shuffle)

    scratch = list(WORK.values())
    strip, send, kept, given, peak = kernel(
        first_kernel,
        (
            shaped(2, GROUPS, SIDE, HALF),
            shaped(N_SCAN, SEND_ROWS, HALF),
            shaped(MODES, 2, 2, HALF, HALF),
            shaped(MODES, 2, 2, HALF, HALF),
            shaped(1, 1),
        ),
        [SMEM, SMEM, HBM, VMEM, VMEM, HBM, HBM],
        scratch,
        out_specs=(VMEM, VMEM, VMEM, VMEM, SMEM),
        name="first",
        limit=30,
    )(info, perm, arrived, modes, amp, right, left)

    chip = (kept + lax.ppermute(given, "scan", SWAP)).reshape(N_SCAN, PRB_ROWS, HALF)
    send = lax.dynamic_update_slice(send, chip, (0, OBJ_ROWS, 0))
    got = exchange(send)
    both = kernel(
        chip_sums_kernel,
        shaped(2, PRB_ROWS, HALF),
        [ANY],
        [pltpu.VMEM((N_SCAN, PRB_ROWS, HALF), F32), pltpu.SemaphoreType.DMA],
        name="sums",
    )(got)
    summed = sum_all(both, "grp", lambda k: shift(N_GRP, k))
    totals = kernel(
        owner_kernel,
        shaped(N_SCAN, SEND_ROWS, HALF),
        [SMEM, SMEM, VMEM],
        [pltpu.VMEM((8, 2, 32, 8, HALF), F32)],
        name="owner",
    )(spots, info, got)
    answer = jnp.broadcast_to(summed[None], (16, 2, PRB_ROWS, HALF)).reshape(N_SCAN, PRB_ROWS, HALF)
    total = exchange(lax.dynamic_update_slice(totals, answer, (0, OBJ_ROWS, 0)))
    other = lax.ppermute(total[:, OBJ_ROWS:], "scan", SWAP)

    moved, kept, given = kernel(
        second_kernel,
        (shaped(96, TILE, HALF), shaped(MODES, 2, 2, HALF, HALF), shaped(MODES, 2, 2, HALF, HALF)),
        [SMEM, SMEM, SMEM, SMEM] + [HBM] * 5 + [VMEM] + [HBM] * 2,
        [
            pltpu.VMEM((MODES, 2, 2, HALF, HALF), F32),
            pltpu.VMEM((MODES, 2, 2, HALF, HALF), F32),
            pltpu.SemaphoreType.DMA((3,)),
            pltpu.VMEM((2, GROUPS, SIDE, HALF), F32),
            pltpu.VMEM((MODES, 2, 2, 2, HALF, HALF), F32),
            pltpu.VMEM((N_SCAN, SEND_ROWS, HALF), F32),
            pltpu.VMEM((N_SCAN, SEND_ROWS, HALF), F32),
            pltpu.VMEM((N_SCAN, PRB_ROWS, HALF), F32),
            pltpu.SemaphoreType.DMA((5,)),
        ]
        + scratch,
        out_specs=(HBM, HBM, HBM),
        name="second",
        limit=48,
    )(info, perm, peak, energy, strip, send, total, other, modes, amp, right, left)
    returned = exchange(moved)

    theirs = lax.ppermute(given, "scan", SWAP).reshape(4, 4, HALF, HALF)
    kept = kept.reshape(4, 4, HALF, HALF)
    mine = sum_turned([kept[k] + theirs[k] for k in range(4)], "grp", lambda k: shift(N_GRP, k))
    mine = sum_turned([mine[k] for k in range(4)], "scan", shift_y)
    mine = sum_all(mine, "scan", shift_z)
    object_new = kernel(
        unpack_kernel,
        shaped(TILE, TILE, HALF),
        [SMEM, SMEM, SMEM, HBM, HBM],
        [
            pltpu.VMEM((TILE + 1, TILE, HALF), F32),
            pltpu.VMEM((96, TILE, HALF), F32),
            pltpu.SemaphoreType.DMA((PARTS + 1,)),
        ],
        out_specs=HBM,
        name="unpack",
        limit=58,
        cost=8 * 1024 * 1024,
    )(spots, info, perm, tiles, returned)
    turns = [lax.ppermute(mine, "scan", shift_y(k)) for k in (1, 2, 3)]
    turns, object_new = lax.optimization_barrier((turns, object_new))
    half = jnp.stack([mine] + turns)
    other_half = lax.ppermute(half, "scan", SWAP)

    half_one = total[:, OBJ_ROWS:].reshape(MODES, 2, 2, HALF, HALF)
    half_one = lax.dynamic_index_in_dim(half_one, band, 0, keepdims=False)
    half_two = lax.dynamic_index_in_dim(other.reshape(MODES, 2, 2, HALF, HALF), band, 0, keepdims=False)
    base = own - in_order(core, half_one, half_two, 0) * PROBE_STEP
    probe_out = kernel(
        finish_kernel,
        shaped(1, 2, SIDE, SIDE),
        [SMEM, VMEM, VMEM, VMEM],
        [pltpu.VMEM((2, 2, SIDE, HALF), F32)],
        name="finish",
    )(info, base, half, other_half)

    object_out = object_new.reshape(TILE, 32, 2, HALF).transpose(0, 2, 1, 3).reshape(TILE, 2, TILE * TILE)
    return object_out, probe_out


def solution(mesh):
    in_specs = (
        P(("grp", "scan"), None, None),
        P(("grp", "scan"), None),
        P(),
        P(("grp", "scan"), None, None),
        P("grp", None, None, None),
    )
    out_specs = (P(("grp", "scan"), None, None), P("grp", None, None, None))
    return jax.shard_map(body, mesh=mesh, in_specs=in_specs, out_specs=out_specs, check_vma=False)
```

```python
import functools
import math

import jax
import jax.numpy as jnp
import ml_dtypes
import numpy as np
from jax import lax
from jax.experimental import pallas as pl
from jax.experimental.pallas import tpu as pltpu
from jax.sharding import PartitionSpec as P

SIDE = 256
HALF = 128
TILE = 64
MODES = 4
PATS = 4
N_SCAN = 32
N_GRP = 4
BAND_ROWS = 32
GROUPS = 5
PROBE_STEP = 0.03125
OBJ_ROWS = 2 * GROUPS * 8
PRB_ROWS = 64
SEND_ROWS = OBJ_ROWS + PRB_ROWS
WEAK = 0.1
F32 = jnp.float32
BF16 = jnp.bfloat16


def row_of_position():
    return np.array([64 * r + 2 * q + h for r in range(2) for h in range(2) for q in range(32)])


def split_table(table):
    high = table.astype(ml_dtypes.bfloat16)
    low = (table - high.astype(np.float64)).astype(ml_dtypes.bfloat16)
    return high, low


def dft_tables():
    j = np.arange(HALF)[None, :]

    def real_form(n, odd):
        angle = 2.0 * math.pi * ((n[:, None] * (2 * j + odd)) % SIDE) / SIDE
        c, s = np.cos(angle) / 16.0, np.sin(angle) / 16.0
        return np.block([[c, -s], [s, c]])

    lanes = np.arange(HALF)
    rows = row_of_position()
    right, left = [], []
    for odd in (0, 1):
        for table in (real_form(lanes, odd), real_form(lanes, odd).T):
            high, low = split_table(table)
            right.append(np.concatenate([high, low], axis=0))
        for table in (real_form(rows, odd).T, real_form(rows, odd)):
            high, low = split_table(table)
            left.append(np.concatenate([high, low], axis=1))
    return np.stack(right), np.stack(left)


def split(x):
    high = x.astype(BF16)
    return high, (x - high.astype(F32)).astype(BF16)


def product(first, second):
    return jnp.dot(first, second, preferred_element_type=F32)


def from_right(pair, at, table, fast):
    high = pair[at, 0]
    if fast:
        return product(high, table[:SIDE])
    return product(high, table[:SIDE]) + product(high, table[SIDE:]) + product(pair[at, 1], table[:SIDE])


def from_left(table, pair, at, fast):
    high = pair[at, 0]
    if fast:
        return product(table[:, :SIDE], high)
    return product(table[:, :SIDE], high) + product(table[:, SIDE:], high) + product(table[:, :SIDE], pair[at, 1])


CHUNK = 16


def chunks(count):
    return [slice(c * CHUNK, (c + 1) * CHUNK) for c in range(count // CHUNK)]


def woven(matrix_tasks, vector_tasks):
    total, done = len(vector_tasks), 0
    for i, task in enumerate(matrix_tasks):
        task()
        upto = total * (i + 1) // len(matrix_tasks)
        for piece in vector_tasks[done:upto]:
            piece()
        done = upto
    if not matrix_tasks:
        for piece in vector_tasks:
            piece()


def gradients(strip, probe, amp, right, left, work, fast):
    sgrad, pgrad, weight, strength = work["sgrad"], work["pgrad"], work["weight"], work["strength"]
    lhs, rhs, far, mid, res, bright = (work[n] for n in ("lhs", "rhs", "far", "mid", "res", "bright"))
    def put_split(ref, at, rows, x):
        if fast:
            ref[at, 0, rows, :] = x.astype(BF16)
        else:
            ref[at, 0, rows, :], ref[at, 1, rows, :] = split(x)

    def one_pattern(p, carry):
        def exit_rows(k):
            def piece(rh, rows):
                full = slice(rh * HALF + rows.start, rh * HALF + rows.stop)
                wave = []
                for u in range(2):
                    o_re, o_im = strip[0, p + u, full, :], strip[1, p + u, full, :]
                    p_re, p_im = probe[k, rh, 0, u, rows, :], probe[k, rh, 1, u, rows, :]
                    wave.append((p_re * o_re - p_im * o_im, p_re * o_im + p_im * o_re))
                put_split(
                    lhs, 2 * (k % 2), full,
                    jnp.concatenate([wave[0][0] + wave[1][0], wave[0][1] + wave[1][1]], axis=1),
                )
                put_split(
                    lhs, 2 * (k % 2) + 1, full,
                    jnp.concatenate([wave[0][0] - wave[1][0], wave[0][1] - wave[1][1]], axis=1),
                )

            return [functools.partial(piece, rh, rows) for rh in range(2) for rows in chunks(HALF)]

        def right_dots(k, back):
            def one(eo):
                at = 2 * (k % 2) + eo
                res[at] = from_right(lhs, at, right[2 * eo + back], fast)

            return [functools.partial(one, eo) for eo in range(2)]

        def fold_rows(k):
            def piece(rows):
                low = slice(HALF + rows.start, HALF + rows.stop)
                at = 2 * (k % 2)
                e_top, e_low, o_top, o_low = res[at, rows, :], res[at, low, :], res[at + 1, rows, :], res[at + 1, low, :]
                for eo in range(2):
                    e = e_top + e_low if eo == 0 else e_top - e_low
                    o = o_top + o_low if eo == 0 else o_top - o_low
                    put_split(rhs, at + eo, rows, jnp.concatenate([e[:, :HALF], o[:, :HALF]], axis=1))
                    put_split(rhs, at + eo, low, jnp.concatenate([e[:, HALF:], o[:, HALF:]], axis=1))

            return [functools.partial(piece, rows) for rows in chunks(HALF)]

        def left_dots(k, back):
            def one(eo):
                at = 2 * (k % 2) + eo
                if back:
                    mid[at] = from_left(left[2 * eo + 1], rhs, at, fast)
                else:
                    far[k, eo] = from_left(left[2 * eo], rhs, at, fast)

            return [functools.partial(one, eo) for eo in range(2)]

        def power_rows(k):
            def piece(eo, rows):
                low = slice(HALF + rows.start, HALF + rows.stop)
                w_re, w_im = far[k, eo, rows, :], far[k, eo, low, :]
                power = w_re * w_re + w_im * w_im
                if k > 0:
                    power = bright[eo, rows, :] + power
                if k == MODES - 1:
                    power = amp[p, eo, rows, :] * lax.rsqrt(power + 1.0)
                bright[eo, rows, :] = power

            return [functools.partial(piece, eo, rows) for eo in range(2) for rows in chunks(HALF)]

        def cut_rows(k):
            def piece(eo, rows):
                low = slice(HALF + rows.start, HALF + rows.stop)
                scale = bright[eo, rows, :]
                put_split(rhs, 2 * (k % 2) + eo, rows, far[k, eo, rows, :] * scale)
                put_split(rhs, 2 * (k % 2) + eo, low, far[k, eo, low, :] * scale)

            return [functools.partial(piece, eo, rows) for eo in range(2) for rows in chunks(HALF)]

        def spread_rows(k):
            def piece(rows):
                low = slice(HALF + rows.start, HALF + rows.stop)
                at = 2 * (k % 2)
                for rh, full in enumerate((rows, low)):
                    if rh == 0:
                        w_re, w_im = mid[at, rows, :] + mid[at + 1, rows, :], mid[at, low, :] + mid[at + 1, low, :]
                    else:
                        w_re, w_im = mid[at, rows, :] - mid[at + 1, rows, :], mid[at, low, :] - mid[at + 1, low, :]
                    put_split(lhs, at, full, jnp.concatenate([w_re[:, :HALF], w_im[:, :HALF]], axis=1))
                    put_split(lhs, at + 1, full, jnp.concatenate([w_re[:, HALF:], w_im[:, HALF:]], axis=1))

            return [functools.partial(piece, rows) for rows in chunks(HALF)]

        def gradient_rows(k):
            def piece(rh, rows):
                full = slice(rh * HALF + rows.start, rh * HALF + rows.stop)
                at = 2 * (k % 2)
                even, odd = res[at, full, :], res[at + 1, full, :]
                for u in range(2):
                    psi = even + odd if u == 0 else even - odd
                    s_re, s_im = psi[:, :HALF], psi[:, HALF:]
                    o_re, o_im = strip[0, p + u, full, :], strip[1, p + u, full, :]
                    p_re, p_im = probe[k, rh, 0, u, rows, :], probe[k, rh, 1, u, rows, :]
                    g_re, g_im = p_re * s_re + p_im * s_im, p_re * s_im - p_im * s_re
                    if k == 0:
                        power = strength[rh, u, rows, :]
                        g_re, g_im = g_re - power * o_re, g_im - power * o_im
                    sgrad[0, p + u, full, :] -= g_re
                    sgrad[1, p + u, full, :] -= g_im
                    pgrad[rh, k, 0, u, rows, :] -= o_re * s_re + o_im * s_im
                    pgrad[rh, k, 1, u, rows, :] -= o_re * s_im - o_im * s_re
                    if k == 0:
                        weight[rh, u, rows, :] += o_re * o_re + o_im * o_im

            return [functools.partial(piece, rh, rows) for rh in range(2) for rows in chunks(HALF)]

        woven([], exit_rows(0))
        woven(right_dots(0, 0), exit_rows(1))
        woven(right_dots(1, 0), fold_rows(0))
        woven(left_dots(0, 0), exit_rows(2))
        woven(right_dots(2, 0), fold_rows(1) + power_rows(0))
        woven(left_dots(1, 0), exit_rows(3))
        woven(right_dots(3, 0), fold_rows(2) + power_rows(1))
        woven(left_dots(2, 0), fold_rows(3))
        woven(left_dots(3, 0), power_rows(2))
        woven([], power_rows(3) + cut_rows(0))
        woven(left_dots(0, 1), cut_rows(1))
        woven(left_dots(1, 1), spread_rows(0))
        woven(right_dots(0, 1), cut_rows(2))
        woven(left_dots(2, 1), spread_rows(1) + gradient_rows(0))
        woven(right_dots(1, 1), cut_rows(3))
        woven(left_dots(3, 1), spread_rows(2) + gradient_rows(1))
        woven(right_dots(2, 1), spread_rows(3))
        woven(right_dots(3, 1), gradient_rows(2))
        woven([], gradient_rows(3))
        return carry

    lax.fori_loop(0, PATS, one_pattern, 0)


WORK = {
    "sgrad": pltpu.VMEM((2, GROUPS, SIDE, HALF), F32),
    "pgrad": pltpu.VMEM((2, MODES, 2, 2, HALF, HALF), F32),
    "weight": pltpu.VMEM((2, 2, HALF, HALF), F32),
    "strength": pltpu.VMEM((2, 2, HALF, HALF), F32),
    "lhs": pltpu.VMEM((4, 2, SIDE, SIDE), BF16),
    "rhs": pltpu.VMEM((4, 2, SIDE, SIDE), BF16),
    "far": pltpu.VMEM((MODES, 2, SIDE, SIDE), F32),
    "mid": pltpu.VMEM((4, SIDE, SIDE), F32),
    "res": pltpu.VMEM((4, SIDE, SIDE), F32),
    "bright": pltpu.VMEM((2, HALF, SIDE), F32),
    "right": pltpu.VMEM((4, 2 * SIDE, SIDE), BF16),
    "left": pltpu.VMEM((4, SIDE, 2 * SIDE), BF16),
    "needed": pltpu.VMEM((4, 2 * GROUPS, TILE, HALF), F32),
    "sems": pltpu.SemaphoreType.DMA((4,)),
}


def hand_over(info, probe, pgrad, weight, kept, given, turned):
    mine = info[2]
    for k in range(MODES):
        mode = (k + info[5]) & 3 if turned else k
        for block in range(4):
            at = (block + info[6]) & 3 if turned else block
            c, u = (at >> 1, at & 1) if turned else (block // 2, block % 2)
            for ref, rh in ((kept, mine), (given, 1 - mine)):
                ref[k, block // 2, block % 2] = pgrad[rh, mode, c, u] + weight[rh, u] * probe[mode, rh, c, u]


def probe_strength(probe, strength):
    most = None
    for rh in range(2):
        for u in range(2):
            for rows in chunks(HALF):
                power = 0.0
                for k in range(MODES):
                    p_re, p_im = probe[k, rh, 0, u, rows, :], probe[k, rh, 1, u, rows, :]
                    power = power + (p_re * p_re + p_im * p_im)
                strength[rh, u, rows, :] = power
                most = power if most is None else jnp.maximum(most, power)
    return jnp.max(most) + 1e-6


def weak_data(strip, strength, energy):
    weak = None
    for p in range(PATS):
        total = 0.0
        for rh in range(2):
            for u in range(2):
                for rows in chunks(HALF):
                    full = slice(rh * HALF + rows.start, rh * HALF + rows.stop)
                    o_re, o_im = strip[0, p + u, full, :], strip[1, p + u, full, :]
                    total = total + strength[rh, u, rows, :] * (o_re * o_re + o_im * o_im)
        small = energy[0, p] < WEAK * WEAK * jnp.sum(total)
        weak = small if weak is None else jnp.logical_and(weak, small)
    return weak


def swap_halves(first, second):
    lane = lax.broadcasted_iota(jnp.int32, first.shape, 1)
    low = lane < TILE
    return (
        jnp.where(low, first, pltpu.roll(second, TILE, 1)),
        jnp.where(low, pltpu.roll(first, TILE, 1), second),
    )


def slot_of(info, perm, r, c):
    row, col = info[0] + r, info[1] + c
    return perm[((row & 7) << 2) + (col & 3)] * 3 + c // 4


def chunk_of(info, r, h, block):
    return (((info[0] + r) & 3) << 3) + h * 4 + block


def clear(work):
    for name in ("sgrad", "pgrad", "weight"):
        work[name][...] = jnp.zeros_like(work[name])


def start_tables(right_in, left_in, work):
    copies = [
        pltpu.make_async_copy(right_in, work["right"], work["sems"].at[0]),
        pltpu.make_async_copy(left_in, work["left"], work["sems"].at[1]),
    ]
    for copy in copies:
        copy.start()
    return copies


def first_kernel(
    info, perm, tiles, probe, amp_in, right_in, left_in, strip, send, kept, given, peak, amp, *scratch
):
    work = dict(zip(WORK, scratch))
    sgrad, pgrad, weight = work["sgrad"], work["pgrad"], work["weight"]
    needed, sem = work["needed"], work["sems"].at[2]
    for r in range(4):
        for c in range(2 * GROUPS):
            pltpu.make_async_copy(tiles.at[slot_of(info, perm, r, c)], needed.at[r, c], sem).start()
    copies = start_tables(right_in, left_in, work)
    copies.append(pltpu.make_async_copy(amp_in, amp, work["sems"].at[3]))
    copies[-1].start()
    clear(work)
    peak[0, 0] = probe_strength(probe, work["strength"])
    pltpu.make_async_copy(needed, needed, sem).wait()
    for r in range(4):
        for g in range(GROUPS):
            for c in range(2):
                one = needed[r, 2 * g, pl.ds(c, 32, stride=2), :]
                two = needed[r, 2 * g + 1, pl.ds(c, 32, stride=2), :]
                top, low = swap_halves(one, two)
                strip[c, g, 64 * r : 64 * r + 32, :] = top
                strip[c, g, 64 * r + 32 : 64 * r + 64, :] = low
    for copy in copies:
        copy.wait()
    gradients(strip, probe, amp, work["right"], work["left"], work, False)
    hand_over(info, probe, pgrad, weight, kept, given, False)
    for r in range(4):
        for h in range(2):
            for block in range(4):
                at = chunk_of(info, r, h, block)
                start = 64 * r + 32 * h + 8 * block
                for c in range(2):
                    for g in range(GROUPS):
                        line = (c * GROUPS + g) * 8
                        send[at, line : line + 8, :] = sgrad[c, g, start : start + 8, :]


def second_kernel(
    info, perm, peak, energy, old_strip, first_in, total_in, other_in, old_probe, amp, right_in, left_in,
    moved, kept_out, given_out, kept, given, out_sems, strip, probe, first_send, total, other, in_sems, *scratch
):
    work = dict(zip(WORK, scratch))
    sgrad, pgrad, weight, out_tiles = work["sgrad"], work["pgrad"], work["weight"], work["needed"]
    pairs = ((old_strip, strip), (total_in, total), (old_probe, probe), (other_in, other), (first_in, first_send))
    come = [pltpu.make_async_copy(a, b, in_sems.at[i]) for i, (a, b) in enumerate(pairs)]
    for copy in come:
        copy.start()
    copies = start_tables(right_in, left_in, work)
    clear(work)
    inverse = 1.0 / peak[0, 0]
    come[0].wait()
    come[1].wait()
    for r in range(4):
        for h in range(2):
            for block in range(4):
                at = chunk_of(info, r, h, block)
                start = 64 * r + 32 * h + 8 * block
                for c in range(2):
                    for g in range(GROUPS):
                        line = (c * GROUPS + g) * 8
                        strip[c, g, start : start + 8, :] -= total[at, line : line + 8, :] * inverse
    mine = info[2]
    come[2].wait()
    come[3].wait()
    for k in range(MODES):
        for c in range(2):
            for u in range(2):
                for part in range(2):
                    piece = ((k * 2 + c) * 2 + u) * 2 + part
                    rows = slice(part * 64, part * 64 + 64)
                    probe[k, mine, c, u, rows, :] -= total[piece, OBJ_ROWS:, :] * PROBE_STEP
                    probe[k, 1 - mine, c, u, rows, :] -= other[piece] * PROBE_STEP
    inverse_now = 1.0 / probe_strength(probe, work["strength"])
    weak = weak_data(strip, work["strength"], energy)
    for copy in copies:
        copy.wait()

    @pl.when(weak)
    def _():
        gradients(strip, probe, amp, work["right"], work["left"], work, True)

    @pl.when(jnp.logical_not(weak))
    def _():
        gradients(strip, probe, amp, work["right"], work["left"], work, False)

    hand_over(info, probe, pgrad, weight, kept, given, True)
    out_copies = [
        pltpu.make_async_copy(given, given_out, out_sems.at[0]),
        pltpu.make_async_copy(kept, kept_out, out_sems.at[1]),
    ]
    for copy in out_copies:
        copy.start()
    come[4].wait()
    for r in range(4):
        for g in range(GROUPS):
            a, b = slot_of(info, perm, r, 2 * g), slot_of(info, perm, r, 2 * g + 1)
            for c in range(2):
                lines = []
                for h in range(2):
                    start = 64 * r + 32 * h
                    line = (c * GROUPS + g) * 8
                    before = jnp.concatenate(
                        [first_send[chunk_of(info, r, h, block), line : line + 8, :] for block in range(4)], axis=0
                    )
                    lines.append(sgrad[c, g, start : start + 32, :] * inverse_now + before * inverse)
                one, two = swap_halves(lines[0], lines[1])
                out_tiles[r, 2 * g, pl.ds(c, 32, stride=2), :] = one
                out_tiles[r, 2 * g + 1, pl.ds(c, 32, stride=2), :] = two
            for col, at in ((2 * g, a), (2 * g + 1, b)):
                pltpu.make_async_copy(out_tiles.at[r, col], moved.at[at], out_sems.at[2]).start()
    for copy in out_copies:
        copy.wait()
    pltpu.make_async_copy(out_tiles, out_tiles, out_sems.at[2]).wait()


def spot_of(spots, t):
    return (spots[t, 0] >> 6) & (BAND_ROWS - 1), spots[t, 1] >> 6


def own_class(info, perm):
    return lax.fori_loop(0, N_SCAN, lambda i, found: jnp.where(perm[i] == info[3], i, found), 0)


def served_slot(spots, cls, t, k):
    row, col = spot_of(spots, t)
    r = ((cls >> 2) - row) & 7
    c = (((cls & 3) - col) & 3) + 4 * k
    valid = jnp.logical_and(r < 4, c < 2 * GROUPS)
    slot = (((row + r) >> 3) << 4) + ((col + c) >> 2)
    return valid, jnp.where(valid, slot, 0)


def pack_kernel(spots, info, perm, tiles, out, sem):
    cls = own_class(info, perm)

    def one(t, carry):
        for k in range(3):
            _, slot = served_slot(spots, cls, t, k)
            pltpu.make_async_copy(tiles.at[slot], out.at[t * 3 + k], sem).start()
        return carry

    lax.fori_loop(0, N_SCAN, one, 0)
    pltpu.make_async_copy(out, out, sem).wait()


PARTS = 4


def unpack_kernel(spots, info, perm, tiles, arrived, out, total, came, sems):
    step = N_SCAN // PARTS
    held = total.at[pl.ds(0, TILE)]
    pltpu.make_async_copy(tiles, held, sems.at[PARTS]).start()
    parts = []
    for part in range(PARTS):
        rows = pl.ds(part * step * 3, step * 3)
        parts.append(pltpu.make_async_copy(arrived.at[rows], came.at[rows], sems.at[part]))
        parts[-1].start()
    cls = own_class(info, perm)
    total[TILE] = jnp.zeros((TILE, HALF), F32)
    pltpu.make_async_copy(tiles, held, sems.at[PARTS]).wait()

    def one(t, carry):
        for k in range(3):
            valid, slot = served_slot(spots, cls, t, k)
            at = jnp.where(valid, slot, TILE)
            total[at] -= came[t * 3 + k]
        return carry

    for part in range(PARTS):
        parts[part].wait()
        lax.fori_loop(part * step, (part + 1) * step, one, 0)
    last = pltpu.make_async_copy(held, out, sems.at[PARTS])
    last.start()
    last.wait()


def owner_kernel(spots, info, arrived, out, band):
    band[...] = jnp.zeros_like(band)
    rho = info[3] >> 3

    def place(t):
        row, col = spot_of(spots, t)
        r = row + ((rho - row) & 3)
        return r >> 2, col >> 1

    def add(t, carry):
        tr, lg = place(t)
        for c in range(2):
            for g in range(GROUPS):
                line = (c * GROUPS + g) * 8
                band[tr, c, lg + g] += arrived[t, line : line + 8, :]
        return carry

    def give(t, carry):
        tr, lg = place(t)
        for c in range(2):
            for g in range(GROUPS):
                line = (c * GROUPS + g) * 8
                out[t, line : line + 8, :] = band[tr, c, lg + g]
        return carry

    lax.fori_loop(0, N_SCAN, add, 0)
    lax.fori_loop(0, N_SCAN, give, 0)


def chip_sums_kernel(arrived, out, rows, sem):
    copy = pltpu.make_async_copy(arrived.at[:, pl.ds(OBJ_ROWS, PRB_ROWS), :], rows, sem)
    copy.start()
    copy.wait()
    for core in range(2):
        for line in range(0, PRB_ROWS, 16):
            total = rows[core, line : line + 16, :]
            for chip in range(1, N_SCAN // 2):
                total = total + rows[2 * chip + core, line : line + 16, :]
            out[core, line : line + 16, :] = total


def finish_kernel(info, base, half, other_half, out, rows):
    for place, ref in ((0, half), (1, other_half)):
        rh = info[2] if place == 0 else 1 - info[2]
        for turn in range(4):
            at = (info[6] - turn) & 3
            c, u = at >> 1, at & 1
            for r in range(2):
                for h in range(2):
                    lines = slice(64 * r + 32 * h, 64 * r + 32 * h + 32)
                    new = base[rh, c, u, lines, :] - ref[turn, lines, :] * PROBE_STEP
                    rows[c, u, pl.ds(rh * HALF + (64 * r + h), 32, stride=2), :] = new
    for c in range(2):
        for u in range(2):
            out[0, c, :, u * HALF : (u + 1) * HALF] = rows[c, u]


def amplitude_kernel(amp, shuffle, out, energy, moved):
    for p in range(PATS):
        x = amp[p]
        energy[0, p] = jnp.sum(x * x)
        first = x.astype(BF16)
        rest = x - first.astype(F32)
        second = rest.astype(BF16)
        third = (rest - second.astype(F32)).astype(BF16)
        total = None
        for piece in (third, second, first):
            part = jnp.dot(piece, shuffle[...], preferred_element_type=F32)
            total = part if total is None else total + part
        for half in range(2):
            moved[half] = total[:, half * HALF : (half + 1) * HALF]
            for eo in range(2):
                out[p, eo, :, half * HALF : (half + 1) * HALF] = moved[half, pl.ds(eo, HALF, stride=2), :]


SMEM = pl.BlockSpec(memory_space=pltpu.SMEM)
VMEM = pl.BlockSpec(memory_space=pltpu.VMEM)
ANY = pl.BlockSpec(memory_space=pl.ANY)
HBM = pl.BlockSpec(memory_space=pltpu.HBM)


def kernel(body, outs, ins, scratch=(), out_specs=None, name=None, limit=20, cost=None):
    return pl.pallas_call(
        body,
        out_shape=outs,
        in_specs=ins,
        out_specs=out_specs if out_specs is not None else jax.tree.map(lambda _: VMEM, outs),
        scratch_shapes=list(scratch),
        compiler_params=pltpu.CompilerParams(vmem_limit_bytes=limit * 1024 * 1024),
        name=name,
        cost_estimate=None if cost is None else pl.CostEstimate(flops=0, bytes_accessed=cost, transcendentals=0),
    )


def shaped(*shape, dtype=F32):
    return jax.ShapeDtypeStruct(shape, dtype)


def shift(n, k):
    return [(i, (i + k) % n) for i in range(n)]


def shift_y(k):
    return [(i, (i & ~6) | ((((i >> 1) & 3) + k) % 4) << 1) for i in range(N_SCAN)]


def shift_z(k):
    return [(i, (i + 8 * k) % N_SCAN) for i in range(N_SCAN)]


SWAP = [(i, i ^ 1) for i in range(N_SCAN)]


def exchange(x):
    return lax.all_to_all(x, "scan", split_axis=0, concat_axis=0, tiled=True)


def sum_turned(parts, axis, perm_of):
    near, far, middle = (lax.ppermute(parts[k], axis, perm_of(k)) for k in (1, 3, 2))
    return (parts[0] + middle) + (near + far)


def sum_all(x, axis, perm_of):
    near, far, middle = (lax.ppermute(x, axis, perm_of(k)) for k in (1, 3, 2))
    return (x + middle) + (near + far)


def gather_rows(x, at, axis, perm_of):
    stacked = jnp.zeros((4,) + x.shape, x.dtype)
    stacked = lax.dynamic_update_index_in_dim(stacked, x, at, 0)
    for k in (1, 3, 2):
        got = lax.ppermute(x, axis, perm_of(k))
        stacked = lax.dynamic_update_index_in_dim(stacked, got, (at - k) % 4, 0)
    return stacked


def in_order(core, mine, theirs, axis):
    return jnp.where(core == 0, jnp.stack([mine, theirs], axis), jnp.stack([theirs, mine], axis))


def body(amplitude, positions, owner_perm, object_tiles, probe):
    band = lax.axis_index("grp")
    me = lax.axis_index("scan")
    core, y_at = me % 2, me // 2 % 4
    right_np, left_np = dft_tables()
    right, left = jnp.asarray(right_np), jnp.asarray(left_np)
    shuffle_np = np.zeros((SIDE, SIDE), np.float32)
    for m in range(SIDE):
        shuffle_np[m, m // 2 + HALF * (m % 2)] = 1.0
    shuffle = jnp.asarray(shuffle_np.astype(ml_dtypes.bfloat16))

    spots = exchange(jnp.broadcast_to(positions[:1, None], (N_SCAN, 1, 2))).reshape(N_SCAN, 2)
    perm = lax.dynamic_index_in_dim(owner_perm, band, 0, keepdims=False)
    spot = positions[0] // TILE
    info = jnp.stack([spot[0] % BAND_ROWS, spot[1], core, me, me, band, y_at]).astype(jnp.int32)

    tiles = object_tiles.reshape(TILE, 2, 32, HALF).transpose(0, 2, 1, 3).reshape(TILE, TILE, HALF)
    packed = kernel(
        pack_kernel,
        shaped(96, TILE, HALF),
        [SMEM, SMEM, SMEM, HBM],
        [pltpu.SemaphoreType.DMA],
        out_specs=HBM,
        name="pack",
    )(spots, info, perm, tiles)
    arrived = exchange(packed)

    own = probe.reshape(2, 2, 2, 32, 2, 2, HALF).transpose(1, 0, 5, 2, 4, 3, 6).reshape(2, 2, 2, HALF, HALF)
    part = gather_rows(lax.dynamic_index_in_dim(own, core, 0, keepdims=False), band, "grp", lambda k: shift(N_GRP, k))
    modes = in_order(core, part, lax.ppermute(part, "scan", SWAP), 1)
    amp, energy = kernel(
        amplitude_kernel,
        (shaped(PATS, 2, HALF, SIDE), shaped(1, PATS)),
        [VMEM, VMEM],
        [pltpu.VMEM((2, SIDE, HALF), F32)],
        out_specs=(VMEM, SMEM),
        name="spread",
    )(amplitude, shuffle)

    scratch = list(WORK.values())
    strip, send, kept, given, peak = kernel(
        first_kernel,
        (
            shaped(2, GROUPS, SIDE, HALF),
            shaped(N_SCAN, SEND_ROWS, HALF),
            shaped(MODES, 2, 2, HALF, HALF),
            shaped(MODES, 2, 2, HALF, HALF),
            shaped(1, 1),
        ),
        [SMEM, SMEM, HBM, VMEM, HBM, HBM, HBM],
        [pltpu.VMEM((PATS, 2, HALF, SIDE), F32)] + scratch,
        out_specs=(VMEM, VMEM, VMEM, VMEM, SMEM),
        name="first",
        limit=38,
    )(info, perm, arrived, modes, amp, right, left)

    chip = (kept + lax.ppermute(given, "scan", SWAP)).reshape(N_SCAN, PRB_ROWS, HALF)
    send = lax.dynamic_update_slice(send, chip, (0, OBJ_ROWS, 0))
    got = exchange(send)
    both = kernel(
        chip_sums_kernel,
        shaped(2, PRB_ROWS, HALF),
        [ANY],
        [pltpu.VMEM((N_SCAN, PRB_ROWS, HALF), F32), pltpu.SemaphoreType.DMA],
        name="sums",
    )(got)
    summed = sum_all(both, "grp", lambda k: shift(N_GRP, k))
    totals = kernel(
        owner_kernel,
        shaped(N_SCAN, SEND_ROWS, HALF),
        [SMEM, SMEM, VMEM],
        [pltpu.VMEM((8, 2, 32, 8, HALF), F32)],
        name="owner",
    )(spots, info, got)
    answer = jnp.broadcast_to(summed[None], (16, 2, PRB_ROWS, HALF)).reshape(N_SCAN, PRB_ROWS, HALF)
    total = exchange(lax.dynamic_update_slice(totals, answer, (0, OBJ_ROWS, 0)))
    other = lax.ppermute(total[:, OBJ_ROWS:], "scan", SWAP)

    moved, kept, given = kernel(
        second_kernel,
        (shaped(96, TILE, HALF), shaped(MODES, 2, 2, HALF, HALF), shaped(MODES, 2, 2, HALF, HALF)),
        [SMEM, SMEM, SMEM, SMEM] + [HBM] * 5 + [VMEM] + [HBM] * 2,
        [
            pltpu.VMEM((MODES, 2, 2, HALF, HALF), F32),
            pltpu.VMEM((MODES, 2, 2, HALF, HALF), F32),
            pltpu.SemaphoreType.DMA((3,)),
            pltpu.VMEM((2, GROUPS, SIDE, HALF), F32),
            pltpu.VMEM((MODES, 2, 2, 2, HALF, HALF), F32),
            pltpu.VMEM((N_SCAN, SEND_ROWS, HALF), F32),
            pltpu.VMEM((N_SCAN, SEND_ROWS, HALF), F32),
            pltpu.VMEM((N_SCAN, PRB_ROWS, HALF), F32),
            pltpu.SemaphoreType.DMA((5,)),
        ]
        + scratch,
        out_specs=(HBM, HBM, HBM),
        name="second",
        limit=48,
    )(info, perm, peak, energy, strip, send, total, other, modes, amp, right, left)
    returned = exchange(moved)

    theirs = lax.ppermute(given, "scan", SWAP).reshape(4, 4, HALF, HALF)
    kept = kept.reshape(4, 4, HALF, HALF)
    mine = sum_turned([kept[k] + theirs[k] for k in range(4)], "grp", lambda k: shift(N_GRP, k))
    mine = sum_turned([mine[k] for k in range(4)], "scan", shift_y)
    mine = sum_all(mine, "scan", shift_z)
    object_new = kernel(
        unpack_kernel,
        shaped(TILE, TILE, HALF),
        [SMEM, SMEM, SMEM, HBM, HBM],
        [
            pltpu.VMEM((TILE + 1, TILE, HALF), F32),
            pltpu.VMEM((96, TILE, HALF), F32),
            pltpu.SemaphoreType.DMA((PARTS + 1,)),
        ],
        out_specs=HBM,
        name="unpack",
        limit=58,
        cost=8 * 1024 * 1024,
    )(spots, info, perm, tiles, returned)
    turns = [lax.ppermute(mine, "scan", shift_y(k)) for k in (1, 2, 3)]
    turns, object_new = lax.optimization_barrier((turns, object_new))
    half = jnp.stack([mine] + turns)
    other_half = lax.ppermute(half, "scan", SWAP)

    half_one = total[:, OBJ_ROWS:].reshape(MODES, 2, 2, HALF, HALF)
    half_one = lax.dynamic_index_in_dim(half_one, band, 0, keepdims=False)
    half_two = lax.dynamic_index_in_dim(other.reshape(MODES, 2, 2, HALF, HALF), band, 0, keepdims=False)
    base = own - in_order(core, half_one, half_two, 0) * PROBE_STEP
    probe_out = kernel(
        finish_kernel,
        shaped(1, 2, SIDE, SIDE),
        [SMEM, VMEM, VMEM, VMEM],
        [pltpu.VMEM((2, 2, SIDE, HALF), F32)],
        name="finish",
    )(info, base, half, other_half)

    object_out = object_new.reshape(TILE, 32, 2, HALF).transpose(0, 2, 1, 3).reshape(TILE, 2, TILE * TILE)
    return object_out, probe_out


def solution(mesh):
    in_specs = (
        P(("grp", "scan"), None, None),
        P(("grp", "scan"), None),
        P(),
        P(("grp", "scan"), None, None),
        P("grp", None, None, None),
    )
    out_specs = (P(("grp", "scan"), None, None), P("grp", None, None, None))
    return jax.shard_map(body, mesh=mesh, in_specs=in_specs, out_specs=out_specs, check_vma=False)
```

```python
import functools
import math

import jax
import jax.numpy as jnp
import ml_dtypes
import numpy as np
from jax import lax
from jax.experimental import pallas as pl
from jax.experimental.pallas import tpu as pltpu
from jax.sharding import PartitionSpec as P

SIDE = 256
HALF = 128
TILE = 64
MODES = 4
PATS = 4
N_SCAN = 32
N_GRP = 4
BAND_ROWS = 32
GROUPS = 5
PROBE_STEP = 0.03125
OBJ_ROWS = 2 * GROUPS * 8
PRB_ROWS = 64
SEND_ROWS = OBJ_ROWS + PRB_ROWS
WEAK = 0.1
F32 = jnp.float32
BF16 = jnp.bfloat16


def row_of_position():
    return np.array([64 * r + 2 * q + h for r in range(2) for h in range(2) for q in range(32)])


def split_table(table):
    high = table.astype(ml_dtypes.bfloat16)
    low = (table - high.astype(np.float64)).astype(ml_dtypes.bfloat16)
    return high, low


def dft_tables():
    j = np.arange(HALF)[None, :]

    def real_form(n, odd):
        angle = 2.0 * math.pi * ((n[:, None] * (2 * j + odd)) % SIDE) / SIDE
        c, s = np.cos(angle) / 16.0, np.sin(angle) / 16.0
        return np.block([[c, -s], [s, c]])

    lanes = np.arange(HALF)
    rows = row_of_position()
    right, left = [], []
    for odd in (0, 1):
        for table in (real_form(lanes, odd), real_form(lanes, odd).T):
            high, low = split_table(table)
            right.append(np.concatenate([high, low], axis=0))
        for table in (real_form(rows, odd).T, real_form(rows, odd)):
            high, low = split_table(table)
            left.append(np.concatenate([high, low], axis=1))
    return np.stack(right), np.stack(left)


def split(x):
    high = x.astype(BF16)
    return high, (x - high.astype(F32)).astype(BF16)


def product(first, second):
    return jnp.dot(first, second, preferred_element_type=F32)


def from_right(pair, at, table, fast):
    high = pair[at, 0]
    if fast:
        return product(high, table[:SIDE])
    return product(high, table[:SIDE]) + product(high, table[SIDE:]) + product(pair[at, 1], table[:SIDE])


def from_left(table, pair, at, fast):
    high = pair[at, 0]
    if fast:
        return product(table[:, :SIDE], high)
    return product(table[:, :SIDE], high) + product(table[:, SIDE:], high) + product(table[:, :SIDE], pair[at, 1])


CHUNK = 16


def chunks(count):
    return [slice(c * CHUNK, (c + 1) * CHUNK) for c in range(count // CHUNK)]


def woven(matrix_tasks, vector_tasks):
    total, done = len(vector_tasks), 0
    for i, task in enumerate(matrix_tasks):
        task()
        upto = total * (i + 1) // len(matrix_tasks)
        for piece in vector_tasks[done:upto]:
            piece()
        done = upto
    if not matrix_tasks:
        for piece in vector_tasks:
            piece()


def gradients(strip, probe, amp, right, left, work, fast, chosen=None):
    sgrad, pgrad, weight, strength = work["sgrad"], work["pgrad"], work["weight"], work["strength"]
    lhs, rhs, far, mid, res, bright = (work[n] for n in ("lhs", "rhs", "far", "mid", "res", "bright"))
    def put_split(ref, at, rows, x):
        if fast:
            ref[at, 0, rows, :] = x.astype(BF16)
        else:
            ref[at, 0, rows, :], ref[at, 1, rows, :] = split(x)

    def one_pattern(p, carry):
        def exit_rows(k):
            def piece(rh, rows):
                full = slice(rh * HALF + rows.start, rh * HALF + rows.stop)
                wave = []
                for u in range(2):
                    o_re, o_im = strip[0, p + u, full, :], strip[1, p + u, full, :]
                    p_re, p_im = probe[k, rh, 0, u, rows, :], probe[k, rh, 1, u, rows, :]
                    wave.append((p_re * o_re - p_im * o_im, p_re * o_im + p_im * o_re))
                put_split(
                    lhs, 2 * (k % 2), full,
                    jnp.concatenate([wave[0][0] + wave[1][0], wave[0][1] + wave[1][1]], axis=1),
                )
                put_split(
                    lhs, 2 * (k % 2) + 1, full,
                    jnp.concatenate([wave[0][0] - wave[1][0], wave[0][1] - wave[1][1]], axis=1),
                )

            return [functools.partial(piece, rh, rows) for rh in range(2) for rows in chunks(HALF)]

        def right_dots(k, back):
            def one(eo):
                at = 2 * (k % 2) + eo
                res[at] = from_right(lhs, at, right[2 * eo + back], fast)

            return [functools.partial(one, eo) for eo in range(2)]

        def fold_rows(k):
            def piece(rows):
                low = slice(HALF + rows.start, HALF + rows.stop)
                at = 2 * (k % 2)
                e_top, e_low, o_top, o_low = res[at, rows, :], res[at, low, :], res[at + 1, rows, :], res[at + 1, low, :]
                for eo in range(2):
                    e = e_top + e_low if eo == 0 else e_top - e_low
                    o = o_top + o_low if eo == 0 else o_top - o_low
                    put_split(rhs, at + eo, rows, jnp.concatenate([e[:, :HALF], o[:, :HALF]], axis=1))
                    put_split(rhs, at + eo, low, jnp.concatenate([e[:, HALF:], o[:, HALF:]], axis=1))

            return [functools.partial(piece, rows) for rows in chunks(HALF)]

        def left_dots(k, back):
            def one(eo):
                at = 2 * (k % 2) + eo
                if back:
                    mid[at] = from_left(left[2 * eo + 1], rhs, at, fast)
                else:
                    far[k, eo] = from_left(left[2 * eo], rhs, at, fast)

            return [functools.partial(one, eo) for eo in range(2)]

        def power_rows(k):
            def piece(eo, rows):
                low = slice(HALF + rows.start, HALF + rows.stop)
                w_re, w_im = far[k, eo, rows, :], far[k, eo, low, :]
                power = w_re * w_re + w_im * w_im
                if k > 0:
                    power = bright[eo, rows, :] + power
                if k == MODES - 1:
                    power = amp[p, eo, rows, :] * lax.rsqrt(power + 1.0)
                bright[eo, rows, :] = power

            return [functools.partial(piece, eo, rows) for eo in range(2) for rows in chunks(HALF)]

        def cut_rows(k):
            def piece(eo, rows):
                low = slice(HALF + rows.start, HALF + rows.stop)
                scale = bright[eo, rows, :]
                put_split(rhs, 2 * (k % 2) + eo, rows, far[k, eo, rows, :] * scale)
                put_split(rhs, 2 * (k % 2) + eo, low, far[k, eo, low, :] * scale)

            return [functools.partial(piece, eo, rows) for eo in range(2) for rows in chunks(HALF)]

        def spread_rows(k):
            def piece(rows):
                low = slice(HALF + rows.start, HALF + rows.stop)
                at = 2 * (k % 2)
                for rh, full in enumerate((rows, low)):
                    if rh == 0:
                        w_re, w_im = mid[at, rows, :] + mid[at + 1, rows, :], mid[at, low, :] + mid[at + 1, low, :]
                    else:
                        w_re, w_im = mid[at, rows, :] - mid[at + 1, rows, :], mid[at, low, :] - mid[at + 1, low, :]
                    put_split(lhs, at, full, jnp.concatenate([w_re[:, :HALF], w_im[:, :HALF]], axis=1))
                    put_split(lhs, at + 1, full, jnp.concatenate([w_re[:, HALF:], w_im[:, HALF:]], axis=1))

            return [functools.partial(piece, rows) for rows in chunks(HALF)]

        def gradient_rows(k):
            def piece(rh, rows):
                full = slice(rh * HALF + rows.start, rh * HALF + rows.stop)
                at = 2 * (k % 2)
                even, odd = res[at, full, :], res[at + 1, full, :]
                for u in range(2):
                    psi = even + odd if u == 0 else even - odd
                    s_re, s_im = psi[:, :HALF], psi[:, HALF:]
                    o_re, o_im = strip[0, p + u, full, :], strip[1, p + u, full, :]
                    p_re, p_im = probe[k, rh, 0, u, rows, :], probe[k, rh, 1, u, rows, :]
                    g_re, g_im = p_re * s_re + p_im * s_im, p_re * s_im - p_im * s_re
                    if k == 0:
                        power = strength[rh, u, rows, :]
                        g_re, g_im = g_re - power * o_re, g_im - power * o_im
                    sgrad[0, p + u, full, :] -= g_re
                    sgrad[1, p + u, full, :] -= g_im
                    pgrad[rh, k, 0, u, rows, :] -= o_re * s_re + o_im * s_im
                    pgrad[rh, k, 1, u, rows, :] -= o_re * s_im - o_im * s_re
                    if k == 0:
                        weight[rh, u, rows, :] += o_re * o_re + o_im * o_im

            return [functools.partial(piece, rh, rows) for rh in range(2) for rows in chunks(HALF)]

        woven([], exit_rows(0))
        woven(right_dots(0, 0), exit_rows(1))
        woven(right_dots(1, 0), fold_rows(0))
        woven(left_dots(0, 0), exit_rows(2))
        woven(right_dots(2, 0), fold_rows(1) + power_rows(0))
        woven(left_dots(1, 0), exit_rows(3))
        woven(right_dots(3, 0), fold_rows(2) + power_rows(1))
        woven(left_dots(2, 0), fold_rows(3))
        woven(left_dots(3, 0), power_rows(2))
        woven([], power_rows(3) + cut_rows(0))
        woven(left_dots(0, 1), cut_rows(1))
        woven(left_dots(1, 1), spread_rows(0))
        woven(right_dots(0, 1), cut_rows(2))
        woven(left_dots(2, 1), spread_rows(1) + gradient_rows(0))
        woven(right_dots(1, 1), cut_rows(3))
        woven(left_dots(3, 1), spread_rows(2) + gradient_rows(1))
        woven(right_dots(2, 1), spread_rows(3))
        woven(right_dots(3, 1), gradient_rows(2))
        woven([], gradient_rows(3))
        return carry

    def one_chosen(p, carry):
        @pl.when(((chosen >> p) & 1) == 1)
        def _():
            one_pattern(p, 0)

        return carry

    lax.fori_loop(0, PATS, one_pattern if chosen is None else one_chosen, 0)


WORK = {
    "sgrad": pltpu.VMEM((2, GROUPS, SIDE, HALF), F32),
    "pgrad": pltpu.VMEM((2, MODES, 2, 2, HALF, HALF), F32),
    "weight": pltpu.VMEM((2, 2, HALF, HALF), F32),
    "strength": pltpu.VMEM((2, 2, HALF, HALF), F32),
    "lhs": pltpu.VMEM((4, 2, SIDE, SIDE), BF16),
    "rhs": pltpu.VMEM((4, 2, SIDE, SIDE), BF16),
    "far": pltpu.VMEM((MODES, 2, SIDE, SIDE), F32),
    "mid": pltpu.VMEM((4, SIDE, SIDE), F32),
    "res": pltpu.VMEM((4, SIDE, SIDE), F32),
    "bright": pltpu.VMEM((2, HALF, SIDE), F32),
    "right": pltpu.VMEM((4, 2 * SIDE, SIDE), BF16),
    "left": pltpu.VMEM((4, SIDE, 2 * SIDE), BF16),
    "needed": pltpu.VMEM((4, 2 * GROUPS, TILE, HALF), F32),
    "sems": pltpu.SemaphoreType.DMA((4,)),
}


def hand_over(info, probe, pgrad, weight, kept, given, turned):
    mine = info[2]
    for k in range(MODES):
        mode = (k + info[5]) & 3 if turned else k
        for block in range(4):
            at = (block + info[6]) & 3 if turned else block
            c, u = (at >> 1, at & 1) if turned else (block // 2, block % 2)
            for ref, rh in ((kept, mine), (given, 1 - mine)):
                ref[k, block // 2, block % 2] = pgrad[rh, mode, c, u] + weight[rh, u] * probe[mode, rh, c, u]


def probe_strength(probe, strength):
    most = None
    for rh in range(2):
        for u in range(2):
            for rows in chunks(HALF):
                power = 0.0
                for k in range(MODES):
                    p_re, p_im = probe[k, rh, 0, u, rows, :], probe[k, rh, 1, u, rows, :]
                    power = power + (p_re * p_re + p_im * p_im)
                strength[rh, u, rows, :] = power
                most = power if most is None else jnp.maximum(most, power)
    return jnp.max(most) + 1e-6


def weak_data(strip, strength, energy):
    weak = 0
    for p in range(PATS):
        total = 0.0
        for rh in range(2):
            for u in range(2):
                for rows in chunks(HALF):
                    full = slice(rh * HALF + rows.start, rh * HALF + rows.stop)
                    o_re, o_im = strip[0, p + u, full, :], strip[1, p + u, full, :]
                    total = total + strength[rh, u, rows, :] * (o_re * o_re + o_im * o_im)
        small = energy[0, p] < WEAK * WEAK * jnp.sum(total)
        weak = weak + jnp.where(small, 1 << p, 0)
    return weak


def swap_halves(first, second):
    lane = lax.broadcasted_iota(jnp.int32, first.shape, 1)
    low = lane < TILE
    return (
        jnp.where(low, first, pltpu.roll(second, TILE, 1)),
        jnp.where(low, pltpu.roll(first, TILE, 1), second),
    )


def slot_of(info, perm, r, c):
    row, col = info[0] + r, info[1] + c
    return perm[((row & 7) << 2) + (col & 3)] * 3 + c // 4


def chunk_of(info, r, h, block):
    return (((info[0] + r) & 3) << 3) + h * 4 + block


def clear(work):
    for name in ("sgrad", "pgrad", "weight"):
        work[name][...] = jnp.zeros_like(work[name])


def start_tables(right_in, left_in, work):
    copies = [
        pltpu.make_async_copy(right_in, work["right"], work["sems"].at[0]),
        pltpu.make_async_copy(left_in, work["left"], work["sems"].at[1]),
    ]
    for copy in copies:
        copy.start()
    return copies


def first_kernel(
    info, perm, tiles, probe, amp_in, right_in, left_in, strip, send, kept, given, peak, amp, *scratch
):
    work = dict(zip(WORK, scratch))
    sgrad, pgrad, weight = work["sgrad"], work["pgrad"], work["weight"]
    needed, sem = work["needed"], work["sems"].at[2]
    for r in range(4):
        for c in range(2 * GROUPS):
            pltpu.make_async_copy(tiles.at[slot_of(info, perm, r, c)], needed.at[r, c], sem).start()
    copies = start_tables(right_in, left_in, work)
    copies.append(pltpu.make_async_copy(amp_in, amp, work["sems"].at[3]))
    copies[-1].start()
    clear(work)
    peak[0, 0] = probe_strength(probe, work["strength"])
    pltpu.make_async_copy(needed, needed, sem).wait()
    for r in range(4):
        for g in range(GROUPS):
            for c in range(2):
                one = needed[r, 2 * g, pl.ds(c, 32, stride=2), :]
                two = needed[r, 2 * g + 1, pl.ds(c, 32, stride=2), :]
                top, low = swap_halves(one, two)
                strip[c, g, 64 * r : 64 * r + 32, :] = top
                strip[c, g, 64 * r + 32 : 64 * r + 64, :] = low
    for copy in copies:
        copy.wait()
    gradients(strip, probe, amp, work["right"], work["left"], work, False)
    hand_over(info, probe, pgrad, weight, kept, given, False)
    for r in range(4):
        for h in range(2):
            for block in range(4):
                at = chunk_of(info, r, h, block)
                start = 64 * r + 32 * h + 8 * block
                for c in range(2):
                    for g in range(GROUPS):
                        line = (c * GROUPS + g) * 8
                        send[at, line : line + 8, :] = sgrad[c, g, start : start + 8, :]


def second_kernel(
    info, perm, peak, energy, old_strip, first_in, total_in, other_in, old_probe, amp, right_in, left_in,
    moved, kept_out, given_out, kept, given, out_sems, strip, probe, first_send, total, other, in_sems, *scratch
):
    work = dict(zip(WORK, scratch))
    sgrad, pgrad, weight, out_tiles = work["sgrad"], work["pgrad"], work["weight"], work["needed"]
    pairs = ((old_strip, strip), (total_in, total), (old_probe, probe), (other_in, other), (first_in, first_send))
    come = [pltpu.make_async_copy(a, b, in_sems.at[i]) for i, (a, b) in enumerate(pairs)]
    for copy in come:
        copy.start()
    copies = start_tables(right_in, left_in, work)
    clear(work)
    inverse = 1.0 / peak[0, 0]
    come[0].wait()
    come[1].wait()
    for r in range(4):
        for h in range(2):
            for block in range(4):
                at = chunk_of(info, r, h, block)
                start = 64 * r + 32 * h + 8 * block
                for c in range(2):
                    for g in range(GROUPS):
                        line = (c * GROUPS + g) * 8
                        strip[c, g, start : start + 8, :] -= total[at, line : line + 8, :] * inverse
    mine = info[2]
    come[2].wait()
    come[3].wait()
    for k in range(MODES):
        for c in range(2):
            for u in range(2):
                for part in range(2):
                    piece = ((k * 2 + c) * 2 + u) * 2 + part
                    rows = slice(part * 64, part * 64 + 64)
                    probe[k, mine, c, u, rows, :] -= total[piece, OBJ_ROWS:, :] * PROBE_STEP
                    probe[k, 1 - mine, c, u, rows, :] -= other[piece] * PROBE_STEP
    inverse_now = 1.0 / probe_strength(probe, work["strength"])
    weak = weak_data(strip, work["strength"], energy)
    for copy in copies:
        copy.wait()

    gradients(strip, probe, amp, work["right"], work["left"], work, True, weak)

    @pl.when(weak != 2**PATS - 1)
    def _():
        gradients(strip, probe, amp, work["right"], work["left"], work, False, 2**PATS - 1 - weak)

    hand_over(info, probe, pgrad, weight, kept, given, True)
    out_copies = [
        pltpu.make_async_copy(given, given_out, out_sems.at[0]),
        pltpu.make_async_copy(kept, kept_out, out_sems.at[1]),
    ]
    for copy in out_copies:
        copy.start()
    come[4].wait()
    for r in range(4):
        for g in range(GROUPS):
            a, b = slot_of(info, perm, r, 2 * g), slot_of(info, perm, r, 2 * g + 1)
            for c in range(2):
                lines = []
                for h in range(2):
                    start = 64 * r + 32 * h
                    line = (c * GROUPS + g) * 8
                    before = jnp.concatenate(
                        [first_send[chunk_of(info, r, h, block), line : line + 8, :] for block in range(4)], axis=0
                    )
                    lines.append(sgrad[c, g, start : start + 32, :] * inverse_now + before * inverse)
                one, two = swap_halves(lines[0], lines[1])
                out_tiles[r, 2 * g, pl.ds(c, 32, stride=2), :] = one
                out_tiles[r, 2 * g + 1, pl.ds(c, 32, stride=2), :] = two
            for col, at in ((2 * g, a), (2 * g + 1, b)):
                pltpu.make_async_copy(out_tiles.at[r, col], moved.at[at], out_sems.at[2]).start()
    for copy in out_copies:
        copy.wait()
    pltpu.make_async_copy(out_tiles, out_tiles, out_sems.at[2]).wait()


def spot_of(spots, t):
    return (spots[t, 0] >> 6) & (BAND_ROWS - 1), spots[t, 1] >> 6


def own_class(info, perm):
    return lax.fori_loop(0, N_SCAN, lambda i, found: jnp.where(perm[i] == info[3], i, found), 0)


def served_slot(spots, cls, t, k):
    row, col = spot_of(spots, t)
    r = ((cls >> 2) - row) & 7
    c = (((cls & 3) - col) & 3) + 4 * k
    valid = jnp.logical_and(r < 4, c < 2 * GROUPS)
    slot = (((row + r) >> 3) << 4) + ((col + c) >> 2)
    return valid, jnp.where(valid, slot, 0)


def pack_kernel(spots, info, perm, tiles, out, sem):
    cls = own_class(info, perm)

    def one(t, carry):
        for k in range(3):
            _, slot = served_slot(spots, cls, t, k)
            pltpu.make_async_copy(tiles.at[slot], out.at[t * 3 + k], sem).start()
        return carry

    lax.fori_loop(0, N_SCAN, one, 0)
    pltpu.make_async_copy(out, out, sem).wait()


PARTS = 4


def unpack_kernel(spots, info, perm, tiles, arrived, out, total, came, sems):
    step = N_SCAN // PARTS
    held = total.at[pl.ds(0, TILE)]
    pltpu.make_async_copy(tiles, held, sems.at[PARTS]).start()
    parts = []
    for part in range(PARTS):
        rows = pl.ds(part * step * 3, step * 3)
        parts.append(pltpu.make_async_copy(arrived.at[rows], came.at[rows], sems.at[part]))
        parts[-1].start()
    cls = own_class(info, perm)
    total[TILE] = jnp.zeros((TILE, HALF), F32)
    pltpu.make_async_copy(tiles, held, sems.at[PARTS]).wait()

    def one(t, carry):
        for k in range(3):
            valid, slot = served_slot(spots, cls, t, k)
            at = jnp.where(valid, slot, TILE)
            total[at] -= came[t * 3 + k]
        return carry

    for part in range(PARTS):
        parts[part].wait()
        lax.fori_loop(part * step, (part + 1) * step, one, 0)
    last = pltpu.make_async_copy(held, out, sems.at[PARTS])
    last.start()
    last.wait()


def owner_kernel(spots, info, arrived, out, band):
    band[...] = jnp.zeros_like(band)
    rho = info[3] >> 3

    def place(t):
        row, col = spot_of(spots, t)
        r = row + ((rho - row) & 3)
        return r >> 2, col >> 1

    def add(t, carry):
        tr, lg = place(t)
        for c in range(2):
            for g in range(GROUPS):
                line = (c * GROUPS + g) * 8
                band[tr, c, lg + g] += arrived[t, line : line + 8, :]
        return carry

    def give(t, carry):
        tr, lg = place(t)
        for c in range(2):
            for g in range(GROUPS):
                line = (c * GROUPS + g) * 8
                out[t, line : line + 8, :] = band[tr, c, lg + g]
        return carry

    lax.fori_loop(0, N_SCAN, add, 0)
    lax.fori_loop(0, N_SCAN, give, 0)


def chip_sums_kernel(arrived, out, rows, sem):
    copy = pltpu.make_async_copy(arrived.at[:, pl.ds(OBJ_ROWS, PRB_ROWS), :], rows, sem)
    copy.start()
    copy.wait()
    for core in range(2):
        for line in range(0, PRB_ROWS, 16):
            total = rows[core, line : line + 16, :]
            for chip in range(1, N_SCAN // 2):
                total = total + rows[2 * chip + core, line : line + 16, :]
            out[core, line : line + 16, :] = total


def finish_kernel(info, base, half, other_half, out, rows):
    for place, ref in ((0, half), (1, other_half)):
        rh = info[2] if place == 0 else 1 - info[2]
        for turn in range(4):
            at = (info[6] - turn) & 3
            c, u = at >> 1, at & 1
            for r in range(2):
                for h in range(2):
                    lines = slice(64 * r + 32 * h, 64 * r + 32 * h + 32)
                    new = base[rh, c, u, lines, :] - ref[turn, lines, :] * PROBE_STEP
                    rows[c, u, pl.ds(rh * HALF + (64 * r + h), 32, stride=2), :] = new
    for c in range(2):
        for u in range(2):
            out[0, c, :, u * HALF : (u + 1) * HALF] = rows[c, u]


def amplitude_kernel(amp, shuffle, out, energy, moved):
    for p in range(PATS):
        x = amp[p]
        energy[0, p] = jnp.sum(x * x)
        first = x.astype(BF16)
        rest = x - first.astype(F32)
        second = rest.astype(BF16)
        third = (rest - second.astype(F32)).astype(BF16)
        total = None
        for piece in (third, second, first):
            part = jnp.dot(piece, shuffle[...], preferred_element_type=F32)
            total = part if total is None else total + part
        for half in range(2):
            moved[half] = total[:, half * HALF : (half + 1) * HALF]
            for eo in range(2):
                out[p, eo, :, half * HALF : (half + 1) * HALF] = moved[half, pl.ds(eo, HALF, stride=2), :]


SMEM = pl.BlockSpec(memory_space=pltpu.SMEM)
VMEM = pl.BlockSpec(memory_space=pltpu.VMEM)
ANY = pl.BlockSpec(memory_space=pl.ANY)
HBM = pl.BlockSpec(memory_space=pltpu.HBM)


def kernel(body, outs, ins, scratch=(), out_specs=None, name=None, limit=20, cost=None):
    return pl.pallas_call(
        body,
        out_shape=outs,
        in_specs=ins,
        out_specs=out_specs if out_specs is not None else jax.tree.map(lambda _: VMEM, outs),
        scratch_shapes=list(scratch),
        compiler_params=pltpu.CompilerParams(vmem_limit_bytes=limit * 1024 * 1024),
        name=name,
        cost_estimate=None if cost is None else pl.CostEstimate(flops=0, bytes_accessed=cost, transcendentals=0),
    )


def shaped(*shape, dtype=F32):
    return jax.ShapeDtypeStruct(shape, dtype)


def shift(n, k):
    return [(i, (i + k) % n) for i in range(n)]


def shift_y(k):
    return [(i, (i & ~6) | ((((i >> 1) & 3) + k) % 4) << 1) for i in range(N_SCAN)]


def shift_z(k):
    return [(i, (i + 8 * k) % N_SCAN) for i in range(N_SCAN)]


SWAP = [(i, i ^ 1) for i in range(N_SCAN)]


def exchange(x):
    return lax.all_to_all(x, "scan", split_axis=0, concat_axis=0, tiled=True)


def sum_turned(parts, axis, perm_of):
    near, far, middle = (lax.ppermute(parts[k], axis, perm_of(k)) for k in (1, 3, 2))
    return (parts[0] + middle) + (near + far)


def sum_all(x, axis, perm_of):
    near, far, middle = (lax.ppermute(x, axis, perm_of(k)) for k in (1, 3, 2))
    return (x + middle) + (near + far)


def gather_rows(x, at, axis, perm_of):
    stacked = jnp.zeros((4,) + x.shape, x.dtype)
    stacked = lax.dynamic_update_index_in_dim(stacked, x, at, 0)
    for k in (1, 3, 2):
        got = lax.ppermute(x, axis, perm_of(k))
        stacked = lax.dynamic_update_index_in_dim(stacked, got, (at - k) % 4, 0)
    return stacked


def in_order(core, mine, theirs, axis):
    return jnp.where(core == 0, jnp.stack([mine, theirs], axis), jnp.stack([theirs, mine], axis))


def body(amplitude, positions, owner_perm, object_tiles, probe):
    band = lax.axis_index("grp")
    me = lax.axis_index("scan")
    core, y_at = me % 2, me // 2 % 4
    right_np, left_np = dft_tables()
    right, left = jnp.asarray(right_np), jnp.asarray(left_np)
    shuffle_np = np.zeros((SIDE, SIDE), np.float32)
    for m in range(SIDE):
        shuffle_np[m, m // 2 + HALF * (m % 2)] = 1.0
    shuffle = jnp.asarray(shuffle_np.astype(ml_dtypes.bfloat16))

    spots = exchange(jnp.broadcast_to(positions[:1, None], (N_SCAN, 1, 2))).reshape(N_SCAN, 2)
    perm = lax.dynamic_index_in_dim(owner_perm, band, 0, keepdims=False)
    spot = positions[0] // TILE
    info = jnp.stack([spot[0] % BAND_ROWS, spot[1], core, me, me, band, y_at]).astype(jnp.int32)

    tiles = object_tiles.reshape(TILE, 2, 32, HALF).transpose(0, 2, 1, 3).reshape(TILE, TILE, HALF)
    packed = kernel(
        pack_kernel,
        shaped(96, TILE, HALF),
        [SMEM, SMEM, SMEM, HBM],
        [pltpu.SemaphoreType.DMA],
        out_specs=HBM,
        name="pack",
    )(spots, info, perm, tiles)
    arrived = exchange(packed)

    own = probe.reshape(2, 2, 2, 32, 2, 2, HALF).transpose(1, 0, 5, 2, 4, 3, 6).reshape(2, 2, 2, HALF, HALF)
    part = gather_rows(lax.dynamic_index_in_dim(own, core, 0, keepdims=False), band, "grp", lambda k: shift(N_GRP, k))
    modes = in_order(core, part, lax.ppermute(part, "scan", SWAP), 1)
    amp, energy = kernel(
        amplitude_kernel,
        (shaped(PATS, 2, HALF, SIDE), shaped(1, PATS)),
        [VMEM, VMEM],
        [pltpu.VMEM((2, SIDE, HALF), F32)],
        out_specs=(VMEM, SMEM),
        name="spread",
    )(amplitude, shuffle)

    scratch = list(WORK.values())
    strip, send, kept, given, peak = kernel(
        first_kernel,
        (
            shaped(2, GROUPS, SIDE, HALF),
            shaped(N_SCAN, SEND_ROWS, HALF),
            shaped(MODES, 2, 2, HALF, HALF),
            shaped(MODES, 2, 2, HALF, HALF),
            shaped(1, 1),
        ),
        [SMEM, SMEM, HBM, VMEM, HBM, HBM, HBM],
        [pltpu.VMEM((PATS, 2, HALF, SIDE), F32)] + scratch,
        out_specs=(VMEM, VMEM, VMEM, VMEM, SMEM),
        name="first",
        limit=38,
    )(info, perm, arrived, modes, amp, right, left)

    chip = (kept + lax.ppermute(given, "scan", SWAP)).reshape(N_SCAN, PRB_ROWS, HALF)
    send = lax.dynamic_update_slice(send, chip, (0, OBJ_ROWS, 0))
    got = exchange(send)
    both = kernel(
        chip_sums_kernel,
        shaped(2, PRB_ROWS, HALF),
        [ANY],
        [pltpu.VMEM((N_SCAN, PRB_ROWS, HALF), F32), pltpu.SemaphoreType.DMA],
        name="sums",
    )(got)
    summed = sum_all(both, "grp", lambda k: shift(N_GRP, k))
    totals = kernel(
        owner_kernel,
        shaped(N_SCAN, SEND_ROWS, HALF),
        [SMEM, SMEM, VMEM],
        [pltpu.VMEM((8, 2, 32, 8, HALF), F32)],
        name="owner",
    )(spots, info, got)
    answer = jnp.broadcast_to(summed[None], (16, 2, PRB_ROWS, HALF)).reshape(N_SCAN, PRB_ROWS, HALF)
    total = exchange(lax.dynamic_update_slice(totals, answer, (0, OBJ_ROWS, 0)))
    other = lax.ppermute(total[:, OBJ_ROWS:], "scan", SWAP)

    moved, kept, given = kernel(
        second_kernel,
        (shaped(96, TILE, HALF), shaped(MODES, 2, 2, HALF, HALF), shaped(MODES, 2, 2, HALF, HALF)),
        [SMEM, SMEM, SMEM, SMEM] + [HBM] * 5 + [VMEM] + [HBM] * 2,
        [
            pltpu.VMEM((MODES, 2, 2, HALF, HALF), F32),
            pltpu.VMEM((MODES, 2, 2, HALF, HALF), F32),
            pltpu.SemaphoreType.DMA((3,)),
            pltpu.VMEM((2, GROUPS, SIDE, HALF), F32),
            pltpu.VMEM((MODES, 2, 2, 2, HALF, HALF), F32),
            pltpu.VMEM((N_SCAN, SEND_ROWS, HALF), F32),
            pltpu.VMEM((N_SCAN, SEND_ROWS, HALF), F32),
            pltpu.VMEM((N_SCAN, PRB_ROWS, HALF), F32),
            pltpu.SemaphoreType.DMA((5,)),
        ]
        + scratch,
        out_specs=(HBM, HBM, HBM),
        name="second",
        limit=48,
    )(info, perm, peak, energy, strip, send, total, other, modes, amp, right, left)
    returned = exchange(moved)

    theirs = lax.ppermute(given, "scan", SWAP).reshape(4, 4, HALF, HALF)
    kept = kept.reshape(4, 4, HALF, HALF)
    mine = sum_turned([kept[k] + theirs[k] for k in range(4)], "grp", lambda k: shift(N_GRP, k))
    mine = sum_turned([mine[k] for k in range(4)], "scan", shift_y)
    mine = sum_all(mine, "scan", shift_z)
    object_new = kernel(
        unpack_kernel,
        shaped(TILE, TILE, HALF),
        [SMEM, SMEM, SMEM, HBM, HBM],
        [
            pltpu.VMEM((TILE + 1, TILE, HALF), F32),
            pltpu.VMEM((96, TILE, HALF), F32),
            pltpu.SemaphoreType.DMA((PARTS + 1,)),
        ],
        out_specs=HBM,
        name="unpack",
        limit=58,
        cost=8 * 1024 * 1024,
    )(spots, info, perm, tiles, returned)
    turns = [lax.ppermute(mine, "scan", shift_y(k)) for k in (1, 2, 3)]
    turns, object_new = lax.optimization_barrier((turns, object_new))
    half = jnp.stack([mine] + turns)
    other_half = lax.ppermute(half, "scan", SWAP)

    half_one = total[:, OBJ_ROWS:].reshape(MODES, 2, 2, HALF, HALF)
    half_one = lax.dynamic_index_in_dim(half_one, band, 0, keepdims=False)
    half_two = lax.dynamic_index_in_dim(other.reshape(MODES, 2, 2, HALF, HALF), band, 0, keepdims=False)
    base = own - in_order(core, half_one, half_two, 0) * PROBE_STEP
    probe_out = kernel(
        finish_kernel,
        shaped(1, 2, SIDE, SIDE),
        [SMEM, VMEM, VMEM, VMEM],
        [pltpu.VMEM((2, 2, SIDE, HALF), F32)],
        name="finish",
    )(info, base, half, other_half)

    object_out = object_new.reshape(TILE, 32, 2, HALF).transpose(0, 2, 1, 3).reshape(TILE, 2, TILE * TILE)
    return object_out, probe_out


def solution(mesh):
    in_specs = (
        P(("grp", "scan"), None, None),
        P(("grp", "scan"), None),
        P(),
        P(("grp", "scan"), None, None),
        P("grp", None, None, None),
    )
    out_specs = (P(("grp", "scan"), None, None), P("grp", None, None, None))
    return jax.shard_map(body, mesh=mesh, in_specs=in_specs, out_specs=out_specs, check_vma=False)
```
